256 devices in a mesh: dp: 16 (over z, core), expert: 16 (over y, x).
Axes of the slice: x: 4, y: 4, z: 8, core: 2. Of those that a mesh axis runs over, the one named last changes fastest.
Arguments:
- tokens: bfloat16 [32768, 1024], P(('dp', 'expert')), may hold values from -6 to 6
- tangent: bfloat16 [32768, 1024], P(('dp', 'expert')), may hold values from -6 to 6
- cotangent: bfloat16 [32768, 1024], P(('dp', 'expert')), may hold values from -6 to 6
- routes: int32 [32768, 2], P(('dp', 'expert')), may hold values from 0 to 15, all different within a row; in each aligned block of 128 rows (0 to 127, 128 to 255, ...) at most 24 rows name the same one
- gate_num: int32 [32768, 2], P(('dp', 'expert')), may hold values from 8 to 56
- w_up: bfloat16 [16, 4096, 1024], P('expert', 'dp'), may hold values from -0.1875 to 0.1875
- w_down: bfloat16 [16, 4096, 1024], P('expert', 'dp'), may hold values from -0.09375 to 0.09375
Outputs:
- hvp: float32 [32768, 1024], P(('dp', 'expert'))
The draws below stay inside these ranges and needn't reach their ends.
Inputs may be any that keep to these rules, and one draw needn't show every extreme that they name: `routes`: the experts of a token are distinct. Within the 128 rows of one device no expert is named by more than 24 rows, and in some device one expert is named by exactly 24 rows.
All inputs are finite; a program needn't handle non-finite values.
Results may differ from the reference program's by a relative error of at most 0.0029.
Values may be sent and summed in bfloat16 or wider, within the bound.
No kernel may reach another device: no remote copies, remote signals or barrier semaphores. Data moves between devices by JAX's collectives and lax.ppermute only.
A program may use at most 192 MiB of HBM per device.

```python
import math
import jax
import jax.numpy as jnp
import numpy as np

D = 1024
FF = 4096
TOPK = 2
TOK_DEV = 128
EXPERTS = 16
TOKENS = 32768
CAP = 24
N_DP = 16
N_EXPERT = 16


def with_ends(values, stream_key, least, high):
    index_at = [jax.random.randint(jax.random.fold_in(stream_key, axis), (), 0, length) for axis, length in enumerate(values.shape)]
    longest = values.shape.index(max(values.shape))
    beside = index_at[:longest] + [(index_at[longest] + 1) % values.shape[longest]] + index_at[longest + 1:]
    return values.at[tuple(index_at)].set(least).at[tuple(beside)].set(high)


def level_of(stream_key, shape, split, low, top_value):
    def one(position, shards_of):
        heights = jax.random.uniform(jax.random.fold_in(jax.random.fold_in(stream_key, 6), position), (shards_of,), jnp.float32, low / len(split), top_value / len(split))
        return jnp.repeat(jnp.exp(heights), shape[position] // shards_of).reshape((-1,) + (1,) * (len(shape) - position - 1))

    level = one(*split[0])
    for cut in split[1:]:
        level = level * one(*cut)
    return level


def routed_block(own_key, own, number, rows, amount, top, most, skew):
    ranking = jax.random.permutation(own_key, amount)
    heavy_load, common = shares(amount, rows * top, most, skew, True), shares(amount, rows * top, most, skew, False)
    places = jnp.arange(amount)

    def named(sizes, offset_by):
        used = int((sizes > 0).sum())
        fixed = max(1, used // 4)
        moved = fixed + (places - fixed + offset_by * (used - fixed)) % max(1, amount - fixed)
        return jnp.zeros((amount,), jnp.int32).at[ranking[jnp.where(places < fixed, places, moved)]].set(jnp.asarray(sizes, jnp.int32))

    sizes = jnp.where(number % 4 == 0, named(heavy_load, number // 4), named(common, number - number // 4 - 1))
    mixed = jax.random.permutation(jax.random.fold_in(own, 3), amount)
    source_of, sink = mixed[0:amount // 2 * 2:2], mixed[1:amount // 2 * 2:2]
    margin = jnp.minimum(sizes[source_of] - 1, most - sizes[sink]) // 2
    margin = jnp.where((source_of == ranking[0]) | (sink == ranking[0]) | (sizes[sink] == 0), 0, jnp.maximum(margin, 0))
    moved = jax.random.randint(jax.random.fold_in(own, 4), (amount // 2,), 0, 1 << 20) % (margin + 1)
    sizes = sizes.at[source_of].add(-moved).at[sink].add(moved)
    labels = jnp.searchsorted(jnp.cumsum(sizes), jnp.arange(rows * top), side="right").astype(jnp.int32)
    listing = labels.reshape(top, rows).T
    listing = listing[jax.random.permutation(jax.random.fold_in(own, 1), rows)]
    offset_by = jax.random.randint(jax.random.fold_in(own, 2), (rows, 1), 0, top)
    return jnp.take_along_axis(listing, (jnp.arange(top)[None, :] + offset_by) % top, axis=1)


def shares(amount, total, most, slope, full):
    loads = [(1 << 20) // math.isqrt(rank ** slope) + 1 for rank in range(1, amount + 1)]
    largest = most if full else min(most, max(-(-total // amount), total * loads[0] // sum(loads)))
    least = 1 if total - largest >= amount - 1 else 0
    given, spare = [largest] + [least] * (amount - 1), total - largest - least * (amount - 1)
    while spare > 0:
        candidates = [i for i in range(1, amount) if given[i] < largest] or [i for i in range(1, amount) if given[i] < most]
        whole, left = sum([loads[i] for i in candidates]), spare
        for i in candidates:
            more = min(most - given[i], max(1, left * loads[i] // whole), spare)
            given[i] = given[i] + more
            spare = spare - more
    return np.array(given)


def centred(own_key, extent, spread, reach, shards=(), held_as=jnp.bfloat16):
    values = spread * jax.random.normal(own_key, extent, jnp.float32)
    if shards:
        values = values * level_of(own_key, extent, shards, -0.22, 0.18)
    return jnp.clip(values, -reach, reach).astype(held_as)


def setup_inputs(seed: int = 0) -> dict:
    key_of = jax.random.split(jax.random.key(seed), 8)
    tokens = centred(key_of[0], (TOKENS, D), 1.0, 6.0, ((0, 256),))
    tangent = centred(key_of[1], (TOKENS, D), 1.0, 6.0, ((0, 256),))
    cotangent = centred(key_of[2], (TOKENS, D), 1.0, 6.0, ((0, 256),))
    routes_keys = jax.random.split(jax.random.fold_in(key_of[3], 1), TOKENS // TOK_DEV)
    routes_turns = jax.random.permutation(jax.random.fold_in(key_of[3], 3), TOKENS // TOK_DEV)
    routes = jax.vmap(lambda own, number: routed_block(jax.random.fold_in(key_of[3], 2), own, number, TOK_DEV, EXPERTS, TOPK, CAP, 2))(routes_keys, routes_turns).reshape((TOKENS, TOPK))
    gate_num = with_ends(jax.random.randint(key_of[4], (TOKENS, TOPK), 8, 57), jax.random.fold_in(key_of[4], 1), 8, 56).astype(jnp.int32)
    w_up = centred(key_of[5], (EXPERTS, FF, D), D ** -0.5, 0.1875, ((0, 16), (1, 16)))
    w_down = centred(key_of[6], (EXPERTS, FF, D), FF ** -0.5, 0.09375, ((0, 16), (1, 16)))
    return dict(tokens=tokens, tangent=tangent, cotangent=cotangent, routes=routes, gate_num=gate_num, w_up=w_up, w_down=w_down)


def curvature(before_act):
    sigma = jax.nn.sigmoid(before_act)
    return sigma * (1.0 - sigma) * (2.0 + before_act * (1.0 - 2.0 * sigma))


def expert_term(rows_in, rows_dir, rows_cot, up_mat, down_mat):
    before_act = jnp.dot(rows_in, up_mat.T, preferred_element_type=jnp.float32)
    lifted = jnp.dot(rows_dir, up_mat.T, preferred_element_type=jnp.float32)
    pulled = jnp.dot(rows_cot, down_mat.T, preferred_element_type=jnp.float32)
    inner = (pulled * curvature(before_act) * lifted).astype(jnp.bfloat16)
    return jnp.dot(inner, up_mat, preferred_element_type=jnp.float32)


def reference(tokens, tangent, cotangent, routes, gate_num, w_up, w_down):
    limit_rows = N_DP * N_EXPERT * CAP
    gates = gate_num.astype(jnp.float32) / 64.0
    result = jnp.zeros(tokens.shape, jnp.float32)
    for expert_id in range(EXPERTS):
        picked = routes == expert_id
        weight = jnp.sum(jnp.where(picked, gates, jnp.zeros_like(gates)), axis=1)
        chosen = jnp.any(picked, axis=1)
        rows_of = jnp.nonzero(chosen, size=limit_rows, fill_value=0)[0].astype(jnp.int32)
        picked_total = jnp.sum(chosen.astype(jnp.int32))
        in_use = jnp.arange(limit_rows, dtype=jnp.int32) < picked_total
        expert_out = expert_term(tokens[rows_of], tangent[rows_of], cotangent[rows_of], w_up[expert_id], w_down[expert_id])
        factor = jnp.where(in_use, weight[rows_of], jnp.zeros_like(weight[rows_of]))
        result = result.at[rows_of].add(factor[:, None] * expert_out)
    return result
```

```python
import functools

import jax
import jax.numpy as jnp
from jax import lax
from jax.experimental import pallas as pl
from jax.experimental.pallas import tpu as pltpu
from jax.sharding import PartitionSpec as P

f32, bf16 = jnp.float32, jnp.bfloat16
CAP = 24
NT = (((1,), (1,)), ((), ()))
VMEM = pl.BlockSpec(memory_space=pltpu.VMEM)


def params(mib):
    return pltpu.CompilerParams(vmem_limit_bytes=mib << 20)


def curvature(x):
    s = jax.nn.sigmoid(x)
    return s * (1.0 - s) * (2.0 + x * (1.0 - 2.0 * s))


def prepare_kernel(slots, routes_ref, routes_t_ref, gates_ref, x_ref, t_ref, c_ref, send_ref, mix_ref):
    n = x_ref.shape[0]
    width = x_ref.shape[1]
    slot = lax.broadcasted_iota(jnp.int32, (slots, n), 0)
    expert = (slot * 2731) >> 16
    place = slot - expert * CAP
    named = (routes_t_ref[0:1, :] == expert) | (routes_t_ref[1:2, :] == expert)
    earlier = lax.broadcasted_iota(jnp.int32, (n, n), 0) < lax.broadcasted_iota(jnp.int32, (n, n), 1)
    named_f = named.astype(f32)
    before = jnp.dot(named_f.astype(bf16), earlier.astype(f32).astype(bf16), preferred_element_type=f32)
    pick = jnp.where(before.astype(jnp.int32) == place, named_f, 0.0).astype(bf16)
    for i, ref in enumerate((x_ref, t_ref, c_ref)):
        send_ref[:, i * width:(i + 1) * width] = jnp.dot(pick, ref[...], preferred_element_type=f32).astype(bf16)
    slot = lax.broadcasted_iota(jnp.int32, (n, slots), 1)
    expert = (slot * 2731) >> 16
    place = slot - expert * CAP
    first, second = routes_ref[:, 0:1] == expert, routes_ref[:, 1:2] == expert
    named_f = (first | second).astype(f32)
    later = lax.broadcasted_iota(jnp.int32, (n, n), 0) > lax.broadcasted_iota(jnp.int32, (n, n), 1)
    before = jnp.dot(later.astype(f32).astype(bf16), named_f.astype(bf16), preferred_element_type=f32)
    gates = gates_ref[...].astype(f32) / 64.0
    weight = jnp.where(first, gates[:, 0:1], 0.0) + jnp.where(second, gates[:, 1:2], 0.0)
    mix_ref[...] = jnp.where(before.astype(jnp.int32) == place, weight, 0.0).astype(bf16)


def prepare(routes, gate_num, tokens, tangent, cotangent, experts):
    n, width = tokens.shape
    slots = experts * CAP
    return pl.pallas_call(
        functools.partial(prepare_kernel, slots),
        out_shape=(
            jax.ShapeDtypeStruct((slots, 3 * width), bf16),
            jax.ShapeDtypeStruct((n, slots), bf16),
        ),
        in_specs=[VMEM] * 6,
        out_specs=(VMEM, VMEM),
        compiler_params=params(16),
    )(routes, routes.T, gate_num, tokens, tangent, cotangent)


def groups_of(refs):
    found = []
    halves = []
    for ref in refs:
        q = 128
        for first in range(0, ref.shape[0], 2 * q):
            halves.append((ref, first))
    for i in range(0, len(halves), 2):
        (ra, ia), (rb, ib) = halves[i], halves[i + 1]
        found.append((ra, ia, rb, ib))
    return found


def expert_kernel(n_w, start, last, *refs):
    own_ref, other_ref = refs[:2]
    w_refs = refs[2:2 + n_w]
    rest = refs[2 + n_w:]
    if not start:
        acc_in, rest = rest[:2], rest[2:]
    out = rest
    q = 128
    width = own_ref.shape[1] // 3
    for g, (ra, ia, rb, ib) in enumerate(groups_of(w_refs)):
        up = jnp.concatenate([ra[ia:ia + q, :], rb[ib:ib + q, :]], axis=0)
        down = jnp.concatenate([ra[ia + q:ia + 2 * q, :], rb[ib + q:ib + 2 * q, :]], axis=0)
        n_g = len(groups_of(w_refs))
        for side, rows_ref in enumerate((own_ref, other_ref)):
            before_act = lax.dot_general(rows_ref[:, :width], up, NT, preferred_element_type=f32)
            lifted = lax.dot_general(rows_ref[:, width:2 * width], up, NT, preferred_element_type=f32)
            pulled = lax.dot_general(rows_ref[:, 2 * width:], down, NT, preferred_element_type=f32)
            inner = (pulled * curvature(before_act) * lifted).astype(bf16)
            part = jnp.dot(inner, up, preferred_element_type=f32)
            if g == 0:
                if not start:
                    part = part + acc_in[side][...]
            else:
                part = part + out[side][...]
            out[side][...] = part.astype(out[side].dtype)


def expert_call(own, other, weights, acc=None, last=False):
    rows, width = own.shape[0], own.shape[1] // 3
    n_w = len(weights)
    acc = () if acc is None else tuple(acc)
    kinds = (f32, bf16) if last else (f32, f32)
    return pl.pallas_call(
        functools.partial(expert_kernel, n_w, not acc, last),
        out_shape=tuple(jax.ShapeDtypeStruct((rows, width), k) for k in kinds),
        in_specs=[VMEM] * (2 + n_w + len(acc)),
        out_specs=(VMEM, VMEM),
        compiler_params=params(40),
    )(own, other, *weights, *acc)


def local(tokens, tangent, cotangent, routes, gate_num, w_up, w_down):
    n_dp = lax.axis_size("dp")
    experts = lax.axis_size("expert")
    width = tokens.shape[1]
    forth = [(i, (i + 2) % n_dp) for i in range(n_dp)]
    back = [(i, (i - 2) % n_dp) for i in range(n_dp)]
    swap = [(i, i ^ 1) for i in range(n_dp)]
    q = 128
    up, down = w_up[0], w_down[0]
    mine = jnp.concatenate([up[:q], down[:q], up[q:], down[q:]], axis=0)
    f1, b1 = lax.ppermute(mine, "dp", forth), lax.ppermute(mine, "dp", back)
    f2, b2 = lax.ppermute(f1, "dp", forth), lax.ppermute(b1, "dp", back)
    f3a, b3b = lax.ppermute(f2[:2 * q], "dp", forth), lax.ppermute(b2[2 * q:], "dp", back)
    f3b, b3a = lax.ppermute(f2[2 * q:], "dp", forth), lax.ppermute(b2[:2 * q], "dp", back)
    f4a, b4b = lax.ppermute(f3a, "dp", forth), lax.ppermute(b3b, "dp", back)

    send, mix = prepare(routes, gate_num, tokens, tangent, cotangent, experts)
    own = lax.all_to_all(send.reshape(experts, CAP, 3 * width), "expert", 0, 0, tiled=True)
    own = own.reshape(experts * CAP, 3 * width)
    other = lax.ppermute(own, "dp", swap)

    acc = expert_call(own, other, (mine, f1, b1))
    acc = expert_call(own, other, (f2, b2), acc)
    acc = expert_call(own, other, (f3a, f3b, b3a, b3b), acc)
    kept, passed = expert_call(own, other, (f4a, b4b), acc, last=True)
    whole = (kept + lax.ppermute(passed, "dp", swap).astype(f32)).astype(bf16)
    returned = lax.all_to_all(whole.reshape(experts, CAP, width), "expert", 0, 0, tiled=True)
    returned = returned.reshape(experts * CAP, width)
    return jnp.dot(mix, returned, preferred_element_type=f32)


def solution(mesh):
    tok = P(("dp", "expert"), None)
    w = P("expert", "dp", None)
    return jax.shard_map(
        local, mesh=mesh, in_specs=(tok,) * 5 + (w, w), out_specs=tok, check_vma=False
    )
```

```python
import functools

import jax
import jax.numpy as jnp
from jax import lax
from jax.experimental import pallas as pl
from jax.experimental.pallas import tpu as pltpu
from jax.sharding import PartitionSpec as P

f32, bf16 = jnp.float32, jnp.bfloat16
CAP = 24
NT = (((1,), (1,)), ((), ()))
VMEM = pl.BlockSpec(memory_space=pltpu.VMEM)


def params(mib):
    return pltpu.CompilerParams(vmem_limit_bytes=mib << 20)


def curvature(x):
    s = jax.nn.sigmoid(x)
    return s * (1.0 - s) * (2.0 + x * (1.0 - 2.0 * s))


def prepare_kernel(slots, routes_ref, routes_t_ref, gates_ref, x_ref, t_ref, c_ref, send_ref, mix_ref):
    n = x_ref.shape[0]
    width = x_ref.shape[1]
    slot = lax.broadcasted_iota(jnp.int32, (slots, n), 0)
    expert = (slot * 2731) >> 16
    place = slot - expert * CAP
    named = (routes_t_ref[0:1, :] == expert) | (routes_t_ref[1:2, :] == expert)
    earlier = lax.broadcasted_iota(jnp.int32, (n, n), 0) < lax.broadcasted_iota(jnp.int32, (n, n), 1)
    named_f = named.astype(f32)
    before = jnp.dot(named_f.astype(bf16), earlier.astype(f32).astype(bf16), preferred_element_type=f32)
    pick = jnp.where(before.astype(jnp.int32) == place, named_f, 0.0).astype(bf16)
    for i, ref in enumerate((x_ref, t_ref, c_ref)):
        send_ref[:, i * width:(i + 1) * width] = jnp.dot(pick, ref[...], preferred_element_type=f32).astype(bf16)
    slot = lax.broadcasted_iota(jnp.int32, (n, slots), 1)
    expert = (slot * 2731) >> 16
    place = slot - expert * CAP
    first, second = routes_ref[:, 0:1] == expert, routes_ref[:, 1:2] == expert
    named_f = (first | second).astype(f32)
    later = lax.broadcasted_iota(jnp.int32, (n, n), 0) > lax.broadcasted_iota(jnp.int32, (n, n), 1)
    before = jnp.dot(later.astype(f32).astype(bf16), named_f.astype(bf16), preferred_element_type=f32)
    gates = gates_ref[...].astype(f32) / 64.0
    weight = jnp.where(first, gates[:, 0:1], 0.0) + jnp.where(second, gates[:, 1:2], 0.0)
    mix_ref[...] = jnp.where(before.astype(jnp.int32) == place, weight, 0.0).astype(bf16)


def prepare(routes, gate_num, tokens, tangent, cotangent, experts):
    n, width = tokens.shape
    slots = experts * CAP
    return pl.pallas_call(
        functools.partial(prepare_kernel, slots),
        out_shape=(
            jax.ShapeDtypeStruct((slots, 3 * width), bf16),
            jax.ShapeDtypeStruct((n, slots), bf16),
        ),
        in_specs=[VMEM] * 6,
        out_specs=(VMEM, VMEM),
        compiler_params=params(16),
    )(routes, routes.T, gate_num, tokens, tangent, cotangent)


def expert_kernel(n_w, start, own_ref, other_ref, *refs):
    ups, downs, rest = refs[:n_w], refs[n_w:2 * n_w], refs[2 * n_w:]
    acc_in, out = ((), rest[-2:]) if start else (rest[:2], rest[-2:])
    width = own_ref.shape[1] // 3
    for side, rows_ref in enumerate((own_ref, other_ref)):
        total = None if start else acc_in[side][...]
        for up_ref, down_ref in zip(ups, downs):
            up, down = up_ref[...], down_ref[...]
            before_act = lax.dot_general(rows_ref[:, :width], up, NT, preferred_element_type=f32)
            lifted = lax.dot_general(rows_ref[:, width:2 * width], up, NT, preferred_element_type=f32)
            pulled = lax.dot_general(rows_ref[:, 2 * width:], down, NT, preferred_element_type=f32)
            inner = (pulled * curvature(before_act) * lifted).astype(bf16)
            part = jnp.dot(inner, up, preferred_element_type=f32)
            total = part if total is None else total + part
        out[side][...] = total.astype(out[side].dtype)


def expert_call(own, other, ups, downs, acc=(), last=False, mark=None):
    rows, width = own.shape[0], own.shape[1] // 3
    kinds = (f32, bf16) if last else (f32, f32)
    operands = (own, other, *ups, *downs, *acc)
    if mark is not None:
        operands += (mark,)
    return pl.pallas_call(
        functools.partial(expert_kernel, len(ups), not acc),
        out_shape=tuple(jax.ShapeDtypeStruct((rows, width), k) for k in kinds),
        in_specs=[VMEM] * len(operands),
        out_specs=(VMEM, VMEM),
        compiler_params=params(24),
    )(*operands)


def hold_kernel(*refs):
    pass


def hold(arrays):
    return pl.pallas_call(
        hold_kernel,
        out_shape=tuple(jax.ShapeDtypeStruct(x.shape, x.dtype) for x in arrays),
        in_specs=[VMEM] * len(arrays),
        out_specs=(VMEM,) * len(arrays),
        input_output_aliases={i: i for i in range(len(arrays))},
        cost_estimate=pl.CostEstimate(flops=200_000_000_000, bytes_accessed=1_000_000_000, transcendentals=0),
    )(*arrays)


def local(tokens, tangent, cotangent, routes, gate_num, w_up, w_down):
    n_dp = lax.axis_size("dp")
    experts = lax.axis_size("expert")
    width = tokens.shape[1]
    forth = [(i, (i + 2) % n_dp) for i in range(n_dp)]
    back = [(i, (i - 2) % n_dp) for i in range(n_dp)]
    swap = [(i, i ^ 1) for i in range(n_dp)]
    up0, down0 = w_up[0], w_down[0]

    def send_on(x, way):
        return lax.ppermute(x, "dp", way)

    uf1, ub1, df1, db1 = send_on(up0, forth), send_on(up0, back), send_on(down0, forth), send_on(down0, back)
    (mark,) = hold((uf1[:16, :128],))
    uf1, ub1, df1, db1, mark = lax.optimization_barrier((uf1, ub1, df1, db1, mark))
    uf2, ub2, df2, db2 = send_on(uf1, forth), send_on(ub1, back), send_on(df1, forth), send_on(db1, back)
    send, mix = prepare(routes, gate_num, tokens, tangent, cotangent, experts)
    own = lax.all_to_all(send.reshape(experts, CAP, 3 * width), "expert", 0, 0, tiled=True)
    own = own.reshape(experts * CAP, 3 * width)
    uf2, ub2, df2, db2, own = lax.optimization_barrier((uf2, ub2, df2, db2, own))
    other = lax.ppermute(own, "dp", swap)
    uf3, db3 = send_on(uf2, forth), send_on(db2, back)
    ub3, df3 = send_on(ub2, back), send_on(df2, forth)
    acc = expert_call(own, other, (up0, uf1, ub1), (down0, df1, db1), mark=mark)
    acc = expert_call(own, other, (uf2, ub2), (df2, db2), acc)
    uf3, db3, ub3, df3, acc = lax.optimization_barrier((uf3, db3, ub3, df3, acc))
    uf4, db4 = send_on(uf3, forth), send_on(db3, back)
    acc = expert_call(own, other, (uf3, ub3), (df3, db3), acc)
    kept, passed = expert_call(own, other, (uf4,), (db4,), acc, last=True)
    whole = (kept + lax.ppermute(passed, "dp", swap).astype(f32)).astype(bf16)
    returned = lax.all_to_all(whole.reshape(experts, CAP, width), "expert", 0, 0, tiled=True)
    returned = returned.reshape(experts * CAP, width)
    return jnp.dot(mix, returned, preferred_element_type=f32)


def solution(mesh):
    tok = P(("dp", "expert"), None)
    w = P("expert", "dp", None)
    return jax.shard_map(
        local, mesh=mesh, in_specs=(tok,) * 5 + (w, w), out_specs=tok, check_vma=False
    )
```

```python
import functools

import jax
import jax.numpy as jnp
from jax import lax
from jax.experimental import pallas as pl
from jax.experimental.pallas import tpu as pltpu
from jax.sharding import PartitionSpec as P

f32, bf16 = jnp.float32, jnp.bfloat16
CAP = 24
NT = (((1,), (1,)), ((), ()))
VMEM = pl.BlockSpec(memory_space=pltpu.VMEM)


def params(mib):
    return pltpu.CompilerParams(vmem_limit_bytes=mib << 20)


def curvature(x):
    s = jax.nn.sigmoid(x)
    return s * (1.0 - s) * (2.0 + x * (1.0 - 2.0 * s))


def prepare_kernel(slots, routes_ref, routes_t_ref, gates_ref, x_ref, t_ref, c_ref, send_ref, mix_ref):
    n = x_ref.shape[0]
    width = x_ref.shape[1]
    slot = lax.broadcasted_iota(jnp.int32, (slots, n), 0)
    expert = (slot * 2731) >> 16
    place = slot - expert * CAP
    named = (routes_t_ref[0:1, :] == expert) | (routes_t_ref[1:2, :] == expert)
    earlier = lax.broadcasted_iota(jnp.int32, (n, n), 0) < lax.broadcasted_iota(jnp.int32, (n, n), 1)
    named_f = named.astype(f32)
    before = jnp.dot(named_f.astype(bf16), earlier.astype(f32).astype(bf16), preferred_element_type=f32)
    pick = jnp.where(before.astype(jnp.int32) == place, named_f, 0.0).astype(bf16)
    for i, ref in enumerate((x_ref, t_ref, c_ref)):
        send_ref[:, i * width:(i + 1) * width] = jnp.dot(pick, ref[...], preferred_element_type=f32).astype(bf16)
    slot = lax.broadcasted_iota(jnp.int32, (n, slots), 1)
    expert = (slot * 2731) >> 16
    place = slot - expert * CAP
    first, second = routes_ref[:, 0:1] == expert, routes_ref[:, 1:2] == expert
    named_f = (first | second).astype(f32)
    later = lax.broadcasted_iota(jnp.int32, (n, n), 0) > lax.broadcasted_iota(jnp.int32, (n, n), 1)
    before = jnp.dot(later.astype(f32).astype(bf16), named_f.astype(bf16), preferred_element_type=f32)
    gates = gates_ref[...].astype(f32) / 64.0
    weight = jnp.where(first, gates[:, 0:1], 0.0) + jnp.where(second, gates[:, 1:2], 0.0)
    mix_ref[...] = jnp.where(before.astype(jnp.int32) == place, weight, 0.0).astype(bf16)


def prepare(routes, gate_num, tokens, tangent, cotangent, experts):
    n, width = tokens.shape
    slots = experts * CAP
    return pl.pallas_call(
        functools.partial(prepare_kernel, slots),
        out_shape=(
            jax.ShapeDtypeStruct((slots, 3 * width), bf16),
            jax.ShapeDtypeStruct((n, slots), bf16),
        ),
        in_specs=[VMEM] * 6,
        out_specs=(VMEM, VMEM),
        compiler_params=params(16),
    )(routes, routes.T, gate_num, tokens, tangent, cotangent)


def expert_kernel(n_w, start, own_ref, other_ref, *refs):
    ups, downs, rest = refs[:n_w], refs[n_w:2 * n_w], refs[2 * n_w:]
    acc_in, out = ((), rest[-2:]) if start else (rest[:2], rest[-2:])
    width = own_ref.shape[1] // 3
    for side, rows_ref in enumerate((own_ref, other_ref)):
        total = None if start else acc_in[side][...]
        for up_ref, down_ref in zip(ups, downs):
            up, down = up_ref[...], down_ref[...]
            before_act = lax.dot_general(rows_ref[:, :width], up, NT, preferred_element_type=f32)
            lifted = lax.dot_general(rows_ref[:, width:2 * width], up, NT, preferred_element_type=f32)
            pulled = lax.dot_general(rows_ref[:, 2 * width:], down, NT, preferred_element_type=f32)
            inner = (pulled * curvature(before_act) * lifted).astype(bf16)
            part = jnp.dot(inner, up, preferred_element_type=f32)
            total = part if total is None else total + part
        out[side][...] = total.astype(out[side].dtype)


def expert_call(own, other, ups, downs, acc=(), last=False, mark=None):
    rows, width = own.shape[0], own.shape[1] // 3
    kinds = (f32, bf16) if last else (f32, f32)
    operands = (own, other, *ups, *downs, *acc)
    if mark is not None:
        operands += (mark,)
    return pl.pallas_call(
        functools.partial(expert_kernel, len(ups), not acc),
        out_shape=tuple(jax.ShapeDtypeStruct((rows, width), k) for k in kinds),
        in_specs=[VMEM] * len(operands),
        out_specs=(VMEM, VMEM),
        compiler_params=params(24),
    )(*operands)


def hold_kernel(*refs):
    pass


def hold(arrays):
    return pl.pallas_call(
        hold_kernel,
        out_shape=tuple(jax.ShapeDtypeStruct(x.shape, x.dtype) for x in arrays),
        in_specs=[VMEM] * len(arrays),
        out_specs=(VMEM,) * len(arrays),
        input_output_aliases={i: i for i in range(len(arrays))},
        cost_estimate=pl.CostEstimate(flops=200_000_000_000, bytes_accessed=1_000_000_000, transcendentals=0),
    )(*arrays)


def local(tokens, tangent, cotangent, routes, gate_num, w_up, w_down):
    n_dp = lax.axis_size("dp")
    experts = lax.axis_size("expert")
    width = tokens.shape[1]
    forth = [(i, (i + 2) % n_dp) for i in range(n_dp)]
    back = [(i, (i - 2) % n_dp) for i in range(n_dp)]
    swap = [(i, i ^ 1) for i in range(n_dp)]
    up0, down0 = w_up[0], w_down[0]

    def send_on(x, way):
        return lax.ppermute(x, "dp", way)

    after = lax.optimization_barrier
    uf1, db1 = send_on(up0, forth), send_on(down0, back)
    df1, ub1 = send_on(down0, forth), send_on(up0, back)
    send, mix = prepare(routes, gate_num, tokens, tangent, cotangent, experts)
    own = lax.all_to_all(send.reshape(experts, CAP, 3 * width), "expert", 0, 0, tiled=True)
    own = own.reshape(experts * CAP, 3 * width)
    (mark,) = hold((uf1[:16, :128],))
    uf1, db1, mark = after((uf1, db1, mark))
    uf2, db2 = send_on(uf1, forth), send_on(db1, back)
    df1, ub1, mark = after((df1, ub1, mark))
    df2, ub2 = send_on(df1, forth), send_on(ub1, back)
    uf2, db2, df1, ub1 = after((uf2, db2, df1, ub1))
    uf3, db3 = send_on(uf2, forth), send_on(db2, back)
    df2, ub2, uf2, db2 = after((df2, ub2, uf2, db2))
    df3, ub3 = send_on(df2, forth), send_on(ub2, back)
    (mark3,) = hold((uf3[:16, :128],))
    uf3, db3, df2, ub2, mark3 = after((uf3, db3, df2, ub2, mark3))
    uf4, db4 = send_on(uf3, forth), send_on(db3, back)
    other = lax.ppermute(own, "dp", swap)
    acc = expert_call(own, other, (up0, uf1, ub1), (down0, df1, db1), mark=mark)
    acc = expert_call(own, other, (uf2, ub2), (df2, db2), acc)
    acc = expert_call(own, other, (uf3, ub3), (df3, db3), acc, mark=mark3)
    kept, passed = expert_call(own, other, (uf4,), (db4,), acc, last=True)
    whole = (kept + lax.ppermute(passed, "dp", swap).astype(f32)).astype(bf16)
    returned = lax.all_to_all(whole.reshape(experts, CAP, width), "expert", 0, 0, tiled=True)
    returned = returned.reshape(experts * CAP, width)
    return jnp.dot(mix, returned, preferred_element_type=f32)


def solution(mesh):
    tok = P(("dp", "expert"), None)
    w = P("expert", "dp", None)
    return jax.shard_map(
        local, mesh=mesh, in_specs=(tok,) * 5 + (w, w), out_specs=tok, check_vma=False
    )
```

```python
import functools

import jax
import jax.numpy as jnp
from jax import lax
from jax.experimental import pallas as pl
from jax.experimental.pallas import tpu as pltpu
from jax.sharding import PartitionSpec as P

f32, bf16 = jnp.float32, jnp.bfloat16
CAP = 24
NT = (((1,), (1,)), ((), ()))
VMEM = pl.BlockSpec(memory_space=pltpu.VMEM)
ANY = pl.BlockSpec(memory_space=pl.ANY)


def params(mib):
    return pltpu.CompilerParams(vmem_limit_bytes=mib << 20)


def curvature(x):
    t = jnp.tanh(0.5 * x)
    return (0.25 - 0.25 * t * t) * (2.0 - x * t)


def prepare_kernel(routes_hbm, gates_hbm, x_hbm, t_hbm, c_hbm, send_hbm, mix_ref, routes, gates, rows, send, sems):
    slots, n = mix_ref.shape
    small = [pltpu.make_async_copy(routes_hbm, routes, sems.at[0]), pltpu.make_async_copy(gates_hbm, gates, sems.at[1])]
    big = [pltpu.make_async_copy(ref, rows.at[i], sems.at[2 + i]) for i, ref in enumerate((x_hbm, t_hbm, c_hbm))]
    width = rows.shape[2]
    leave = [
        pltpu.make_async_copy(send.at[i], send_hbm.at[:, i * width:(i + 1) * width], sems.at[5 + i]) for i in range(3)
    ]
    for copy in small + big:
        copy.start()
    for copy in small:
        copy.wait()
    slot = lax.broadcasted_iota(jnp.int32, (slots, n), 0)
    expert = (slot * 2731) >> 16
    place = slot - expert * CAP
    first, second = routes[0:1, :] == expert, routes[1:2, :] == expert
    named = (first | second).astype(f32)
    earlier = lax.broadcasted_iota(jnp.int32, (n, n), 0) < lax.broadcasted_iota(jnp.int32, (n, n), 1)
    before = jnp.dot(named.astype(bf16), earlier.astype(f32).astype(bf16), preferred_element_type=f32)
    here = before.astype(jnp.int32) == place
    pick = jnp.where(here, named, 0.0).astype(bf16)
    for i in range(3):
        big[i].wait()
        send[i] = jnp.dot(pick, rows[i], preferred_element_type=f32).astype(bf16)
        leave[i].start()
    weights = gates[...].astype(f32) / 64.0
    weight = jnp.where(first, weights[0:1, :], 0.0) + jnp.where(second, weights[1:2, :], 0.0)
    mix_ref[...] = jnp.where(here, weight, 0.0).astype(bf16)
    for copy in leave:
        copy.wait()


def prepare(routes, gate_num, tokens, tangent, cotangent, experts):
    n, width = tokens.shape
    slots = experts * CAP
    return pl.pallas_call(
        prepare_kernel,
        out_shape=(
            jax.ShapeDtypeStruct((slots, 3 * width), bf16),
            jax.ShapeDtypeStruct((slots, n), bf16),
        ),
        in_specs=[ANY] * 5,
        out_specs=(ANY, VMEM),
        scratch_shapes=[
            pltpu.VMEM((2, n), jnp.int32),
            pltpu.VMEM((2, n), jnp.int32),
            pltpu.VMEM((3, n, width), bf16),
            pltpu.VMEM((3, slots, width), bf16),
            pltpu.SemaphoreType.DMA((8,)),
        ],
        compiler_params=params(16),
    )(*(pltpu.with_memory_space_constraint(a, pltpu.HBM) for a in (routes.T, gate_num.T, tokens, tangent, cotangent)))


def inner_of(rows_ref, up, down):
    width = up.shape[1]
    before_act = lax.dot_general(rows_ref[:, :width], up, NT, preferred_element_type=f32)
    lifted = lax.dot_general(rows_ref[:, width:2 * width], up, NT, preferred_element_type=f32)
    pulled = lax.dot_general(rows_ref[:, 2 * width:], down, NT, preferred_element_type=f32)
    return (pulled * curvature(before_act) * lifted).astype(bf16)


def first_kernel(n_w, own_ref, other_ref, *refs):
    ups, downs = refs[:n_w], refs[n_w:2 * n_w]
    acc_own, acc_other, own_out, other_out, up_buf, down_buf, sems = refs[-7:]
    width = up_buf.shape[2]
    copies = {}

    def fetch(key, source, target):
        copies[key] = pltpu.make_async_copy(source, target, sems.at[len(copies)])
        copies[key].start()

    def take_rows(side, source, target):
        for i in range(3):
            part = slice(i * width, (i + 1) * width)
            fetch((side, i), source.at[:, part], target.at[:, part])

    fetch(("up", 0), ups[0], up_buf.at[0])
    take_rows(0, own_ref, own_out)
    fetch(("down", 0), downs[0], down_buf.at[0])
    for g in range(1, n_w):
        fetch(("up", g), ups[g], up_buf.at[g])
        fetch(("down", g), downs[g], down_buf.at[g])
    take_rows(1, other_ref, other_out)
    for side, (rows_ref, acc_ref) in enumerate(((own_out, acc_own), (other_out, acc_other))):
        for i in range(3):
            copies[side, i].wait()
        inners = []
        for g in range(n_w):
            if side == 0:
                copies["up", g].wait()
                copies["down", g].wait()
            inners.append(inner_of(rows_ref, up_buf[g], down_buf[g]))
        total = None
        for g, inner in enumerate(inners):
            part = jnp.dot(inner, up_buf[g], preferred_element_type=f32)
            total = part if total is None else total + part
        acc_ref[...] = total


def first_call(own, other, ups, downs, mark):
    rows, width = own.shape[0], own.shape[1] // 3
    n_w = len(ups)
    operands = (own, other, *ups, *downs, mark)
    return pl.pallas_call(
        functools.partial(first_kernel, n_w),
        out_shape=(
            jax.ShapeDtypeStruct((rows, width), f32),
            jax.ShapeDtypeStruct((rows, width), f32),
            jax.ShapeDtypeStruct(own.shape, bf16),
            jax.ShapeDtypeStruct(own.shape, bf16),
        ),
        in_specs=[ANY] * len(operands),
        out_specs=(VMEM,) * 4,
        scratch_shapes=[
            pltpu.VMEM((n_w, *ups[0].shape), bf16),
            pltpu.VMEM((n_w, *ups[0].shape), bf16),
            pltpu.SemaphoreType.DMA((2 * n_w + 6,)),
        ],
        compiler_params=params(28),
    )(*operands)


def next_kernel(n_w, own_ref, other_ref, *refs):
    ups, downs, acc_in, out = refs[:n_w], refs[n_w:2 * n_w], refs[2 * n_w:2 * n_w + 2], refs[-2:]
    for side, rows_ref in enumerate((own_ref, other_ref)):
        inners = [inner_of(rows_ref, up[...], down[...]) for up, down in zip(ups, downs)]
        total = acc_in[side][...]
        for inner, up in zip(inners, ups):
            total = total + jnp.dot(inner, up[...], preferred_element_type=f32)
        out[side][...] = total.astype(out[side].dtype)


def next_call(own, other, ups, downs, acc, last=False, mark=None):
    rows, width = own.shape[0], own.shape[1] // 3
    kinds = (f32, bf16) if last else (f32, f32)
    operands = tuple(pltpu.with_memory_space_constraint(x, pltpu.VMEM) for x in (own, other, *ups, *downs, *acc))
    specs = [VMEM] * len(operands)
    if mark is not None:
        operands, specs = operands + (mark,), specs + [ANY]
    return pl.pallas_call(
        functools.partial(next_kernel, len(ups)),
        out_shape=tuple(jax.ShapeDtypeStruct((rows, width), k) for k in kinds),
        in_specs=specs,
        out_specs=(VMEM, VMEM),
        compiler_params=params(24),
    )(*operands)


def hold_kernel(x_ref, mark_ref):
    mark_ref[...] = jnp.zeros_like(mark_ref)


def hold(x):
    return pl.pallas_call(
        hold_kernel,
        out_shape=jax.ShapeDtypeStruct((8, 128), f32),
        in_specs=[ANY],
        out_specs=VMEM,
        compiler_params=params(1),
        cost_estimate=pl.CostEstimate(flops=200_000_000_000, bytes_accessed=1_000_000_000, transcendentals=0),
    )(x)


def local(tokens, tangent, cotangent, routes, gate_num, w_up, w_down):
    n_dp = lax.axis_size("dp")
    experts = lax.axis_size("expert")
    width = tokens.shape[1]
    forth = [(i, (i + 2) % n_dp) for i in range(n_dp)]
    back = [(i, (i - 2) % n_dp) for i in range(n_dp)]
    swap = [(i, i ^ 1) for i in range(n_dp)]
    up0, down0 = w_up[0], w_down[0]

    def send_on(x, way):
        return lax.ppermute(x, "dp", way)

    after = lax.optimization_barrier
    uf1, db1 = send_on(up0, forth), send_on(down0, back)
    df1, ub1 = send_on(down0, forth), send_on(up0, back)
    send, mix = prepare(routes, gate_num, tokens, tangent, cotangent, experts)
    own = lax.all_to_all(send.reshape(experts, CAP, 3 * width), "expert", 0, 0, tiled=True)
    own = own.reshape(experts * CAP, 3 * width)
    mark = hold(uf1)
    uf1, db1, mark = after((uf1, db1, mark))
    uf2, db2 = send_on(uf1, forth), send_on(db1, back)
    df1, ub1, mark = after((df1, ub1, mark))
    df2, ub2 = send_on(df1, forth), send_on(ub1, back)
    uf2, db2, df1, ub1 = after((uf2, db2, df1, ub1))
    uf3, db3 = send_on(uf2, forth), send_on(db2, back)
    df2, ub2, uf2, db2 = after((df2, ub2, uf2, db2))
    df3, ub3 = send_on(df2, forth), send_on(ub2, back)
    mark3 = hold(uf3)
    uf3, db3, df2, ub2, mark3 = after((uf3, db3, df2, ub2, mark3))
    uf4, db4 = send_on(uf3, forth), send_on(db3, back)
    other = lax.ppermute(own, "dp", swap)
    *acc, own, other = first_call(own, other, (up0, uf1, ub1, uf2, ub2), (down0, df1, db1, df2, db2), mark)
    acc = next_call(own, other, (uf3, ub3), (df3, db3), acc, mark=mark3)
    kept, passed = next_call(own, other, (uf4,), (db4,), acc, last=True)
    whole = (kept + lax.ppermute(passed, "dp", swap).astype(f32)).astype(bf16)
    returned = lax.all_to_all(whole.reshape(experts, CAP, width), "expert", 0, 0, tiled=True)
    returned = returned.reshape(experts * CAP, width)
    return lax.dot_general(mix, returned, (((0,), (0,)), ((), ())), preferred_element_type=f32)


def solution(mesh):
    tok = P(("dp", "expert"), None)
    w = P("expert", "dp", None)
    return jax.shard_map(
        local, mesh=mesh, in_specs=(tok,) * 5 + (w, w), out_specs=tok, check_vma=False
    )
```

```python
import functools

import jax
import jax.numpy as jnp
from jax import lax
from jax.experimental import pallas as pl
from jax.experimental.pallas import tpu as pltpu
from jax.sharding import PartitionSpec as P

f32, bf16 = jnp.float32, jnp.bfloat16
CAP = 24
NT = (((1,), (1,)), ((), ()))
VMEM = pl.BlockSpec(memory_space=pltpu.VMEM)
ANY = pl.BlockSpec(memory_space=pl.ANY)


def params(mib):
    return pltpu.CompilerParams(vmem_limit_bytes=mib << 20)


def curvature(x):
    t = jnp.tanh(0.5 * x)
    return (0.25 - 0.25 * t * t) * (2.0 - x * t)


def prepare_kernel(routes_hbm, gates_hbm, x_hbm, t_hbm, c_hbm, send_hbm, mix_ref, routes, gates, rows, send, sems):
    slots, n = mix_ref.shape
    small = [pltpu.make_async_copy(routes_hbm, routes, sems.at[0]), pltpu.make_async_copy(gates_hbm, gates, sems.at[1])]
    big = [pltpu.make_async_copy(ref, rows.at[i], sems.at[2 + i]) for i, ref in enumerate((x_hbm, t_hbm, c_hbm))]
    width = rows.shape[2]
    leave = [
        pltpu.make_async_copy(send.at[i], send_hbm.at[:, i * width:(i + 1) * width], sems.at[5 + i]) for i in range(3)
    ]
    for copy in small + big:
        copy.start()
    for copy in small:
        copy.wait()
    slot = lax.broadcasted_iota(jnp.int32, (slots, n), 0)
    expert = (slot * 2731) >> 16
    place = slot - expert * CAP
    first, second = routes[0:1, :] == expert, routes[1:2, :] == expert
    named = (first | second).astype(f32)
    earlier = lax.broadcasted_iota(jnp.int32, (n, n), 0) < lax.broadcasted_iota(jnp.int32, (n, n), 1)
    before = jnp.dot(named.astype(bf16), earlier.astype(f32).astype(bf16), preferred_element_type=f32)
    here = before.astype(jnp.int32) == place
    pick = jnp.where(here, named, 0.0).astype(bf16)
    for i in range(3):
        big[i].wait()
        send[i] = jnp.dot(pick, rows[i], preferred_element_type=f32).astype(bf16)
        leave[i].start()
    weights = gates[...].astype(f32) / 64.0
    weight = jnp.where(first, weights[0:1, :], 0.0) + jnp.where(second, weights[1:2, :], 0.0)
    mix_ref[...] = jnp.where(here, weight, 0.0).astype(bf16)
    for copy in leave:
        copy.wait()


def prepare(routes, gate_num, tokens, tangent, cotangent, experts):
    n, width = tokens.shape
    slots = experts * CAP
    return pl.pallas_call(
        prepare_kernel,
        out_shape=(
            jax.ShapeDtypeStruct((slots, 3 * width), bf16),
            jax.ShapeDtypeStruct((slots, n), bf16),
        ),
        in_specs=[ANY] * 5,
        out_specs=(ANY, VMEM),
        scratch_shapes=[
            pltpu.VMEM((2, n), jnp.int32),
            pltpu.VMEM((2, n), jnp.int32),
            pltpu.VMEM((3, n, width), bf16),
            pltpu.VMEM((3, slots, width), bf16),
            pltpu.SemaphoreType.DMA((8,)),
        ],
        compiler_params=params(16),
    )(*(pltpu.with_memory_space_constraint(a, pltpu.HBM) for a in (routes.T, gate_num.T, tokens, tangent, cotangent)))


def inner_of(rows_ref, up, down):
    width = up.shape[1]
    before_act = lax.dot_general(rows_ref[:, :width], up, NT, preferred_element_type=f32)
    lifted = lax.dot_general(rows_ref[:, width:2 * width], up, NT, preferred_element_type=f32)
    pulled = lax.dot_general(rows_ref[:, 2 * width:], down, NT, preferred_element_type=f32)
    return (pulled * curvature(before_act) * lifted).astype(bf16)


class Fetcher:
    def __init__(self, jobs, sems):
        self.copies = {key: pltpu.make_async_copy(src, dst, sems.at[i]) for i, (key, src, dst) in enumerate(jobs)}
        self.queue = list(self.copies)

    def start(self, count):
        for key in self.queue[:count]:
            self.copies[key].start()
        del self.queue[:count]

    def wait(self, *keys):
        for key in keys:
            self.copies[key].wait()


def first_kernel(n_w, own_ref, other_ref, *refs):
    ups, downs = refs[:n_w], refs[n_w:2 * n_w]
    acc_own, acc_other, own_out, other_out, up_buf, down_buf, sems = refs[-7:]
    width = up_buf.shape[2]

    def thirds(side, source, target):
        parts = [slice(i * width, (i + 1) * width) for i in range(3)]
        return [((side, i), source.at[:, part], target.at[:, part]) for i, part in enumerate(parts)]

    weights = [[(("up", g), ups[g], up_buf.at[g]), (("down", g), downs[g], down_buf.at[g])] for g in range(n_w)]
    own_jobs, other_jobs = thirds(0, own_ref, own_out), thirds(1, other_ref, other_out)
    jobs = [weights[0][0], *own_jobs, weights[0][1]]
    for g in range(1, n_w):
        jobs += weights[g]
    jobs += other_jobs
    fetcher = Fetcher(jobs, sems)
    fetcher.start(7)
    for side, (rows_ref, acc_ref) in enumerate(((own_out, acc_own), (other_out, acc_other))):
        if side:
            fetcher.wait((1, 0), (1, 1), (1, 2))
        inners = []
        for g in range(n_w):
            if not side:
                fetcher.wait(*([(0, 0), (0, 1), (0, 2)] if not g else []), ("up", g), ("down", g))
                fetcher.start(3)
            inners.append(inner_of(rows_ref, up_buf[g], down_buf[g]))
        total = None
        for g, inner in enumerate(inners):
            part = jnp.dot(inner, up_buf[g], preferred_element_type=f32)
            total = part if total is None else total + part
        acc_ref[...] = total


def first_call(own, other, ups, downs, mark):
    rows, width = own.shape[0], own.shape[1] // 3
    n_w = len(ups)
    operands = (own, other, *ups, *downs, mark)
    return pl.pallas_call(
        functools.partial(first_kernel, n_w),
        out_shape=(
            jax.ShapeDtypeStruct((rows, width), f32),
            jax.ShapeDtypeStruct((rows, width), f32),
            jax.ShapeDtypeStruct(own.shape, bf16),
            jax.ShapeDtypeStruct(own.shape, bf16),
        ),
        in_specs=[ANY] * len(operands),
        out_specs=(VMEM,) * 4,
        scratch_shapes=[
            pltpu.VMEM((n_w, *ups[0].shape), bf16),
            pltpu.VMEM((n_w, *ups[0].shape), bf16),
            pltpu.SemaphoreType.DMA((2 * n_w + 6,)),
        ],
        compiler_params=params(28),
    )(*operands)


def next_kernel(n_rows, n_w, *refs):
    rows, ups, downs = refs[:n_rows], refs[n_rows:n_rows + n_w], refs[n_rows + n_w:n_rows + 2 * n_w]
    acc_in, out = refs[n_rows + 2 * n_w:2 * n_rows + 2 * n_w], refs[-n_rows - 3:-3]
    up_buf, down_buf, sems = refs[-3:]
    jobs = []
    for g in range(n_w):
        jobs += [(("up", g), ups[g], up_buf.at[g]), (("down", g), downs[g], down_buf.at[g])]
    fetcher = Fetcher(jobs, sems)
    fetcher.start(2 * n_w)
    for side, rows_ref in enumerate(rows):
        inners = []
        for g in range(n_w):
            if not side:
                fetcher.wait(("up", g), ("down", g))
            inners.append(inner_of(rows_ref, up_buf[g], down_buf[g]))
        total = acc_in[side][...]
        for g, inner in enumerate(inners):
            total = total + jnp.dot(inner, up_buf[g], preferred_element_type=f32)
        out[side][...] = total.astype(out[side].dtype)


def next_call(rows, ups, downs, acc, mark):
    n_w = len(ups)
    inside = [pltpu.with_memory_space_constraint(x, pltpu.VMEM) for x in (*rows, *acc)]
    operands = (*inside[:len(rows)], *ups, *downs, *inside[len(rows):], mark)
    return pl.pallas_call(
        functools.partial(next_kernel, len(rows), n_w),
        out_shape=tuple(jax.ShapeDtypeStruct(x.shape, f32) for x in acc),
        in_specs=[VMEM] * len(rows) + [ANY] * (2 * n_w) + [VMEM] * len(acc) + [ANY],
        out_specs=(VMEM,) * len(acc),
        scratch_shapes=[
            pltpu.VMEM((n_w, *ups[0].shape), bf16),
            pltpu.VMEM((n_w, *ups[0].shape), bf16),
            pltpu.SemaphoreType.DMA((2 * n_w,)),
        ],
        compiler_params=params(24),
    )(*operands)


def last_kernel(rows_ref, up_ref, down_ref, acc_ref, out_ref):
    inner = inner_of(rows_ref, up_ref[...], down_ref[...])
    total = acc_ref[...] + jnp.dot(inner, up_ref[...], preferred_element_type=f32)
    out_ref[...] = total.astype(out_ref.dtype)


def last_call(rows, up, down, acc, kind):
    operands = tuple(pltpu.with_memory_space_constraint(x, pltpu.VMEM) for x in (rows, up, down, acc))
    return pl.pallas_call(
        last_kernel,
        out_shape=jax.ShapeDtypeStruct(acc.shape, kind),
        in_specs=[VMEM] * 4,
        out_specs=VMEM,
        compiler_params=params(16),
    )(*operands)


def hold_kernel(x_ref, mark_ref):
    mark_ref[...] = jnp.zeros_like(mark_ref)


def hold(x):
    return pl.pallas_call(
        hold_kernel,
        out_shape=jax.ShapeDtypeStruct((8, 128), f32),
        in_specs=[ANY],
        out_specs=VMEM,
        compiler_params=params(1),
        cost_estimate=pl.CostEstimate(flops=200_000_000_000, bytes_accessed=1_000_000_000, transcendentals=0),
    )(x)


def local(tokens, tangent, cotangent, routes, gate_num, w_up, w_down):
    n_dp = lax.axis_size("dp")
    experts = lax.axis_size("expert")
    width = tokens.shape[1]
    forth = [(i, (i + 2) % n_dp) for i in range(n_dp)]
    back = [(i, (i - 2) % n_dp) for i in range(n_dp)]
    swap = [(i, i ^ 1) for i in range(n_dp)]
    up0, down0 = w_up[0], w_down[0]

    def send_on(x, way):
        return lax.ppermute(x, "dp", way)

    after = lax.optimization_barrier
    uf1, db1 = send_on(up0, forth), send_on(down0, back)
    df1, ub1 = send_on(down0, forth), send_on(up0, back)
    send, mix = prepare(routes, gate_num, tokens, tangent, cotangent, experts)
    own = lax.all_to_all(send.reshape(experts, CAP, 3 * width), "expert", 0, 0, tiled=True)
    own = own.reshape(experts * CAP, 3 * width)
    mark = hold(uf1)
    uf1, db1, mark = after((uf1, db1, mark))
    uf2, db2 = send_on(uf1, forth), send_on(db1, back)
    df1, ub1, mark = after((df1, ub1, mark))
    df2, ub2 = send_on(df1, forth), send_on(ub1, back)
    uf2, db2, df1, ub1 = after((uf2, db2, df1, ub1))
    uf3, db3 = send_on(uf2, forth), send_on(db2, back)
    df2, ub2, uf2, db2 = after((df2, ub2, uf2, db2))
    df3, ub3 = send_on(df2, forth), send_on(ub2, back)
    mark3 = hold(uf3)
    uf3, db3, df2, ub2, mark3 = after((uf3, db3, df2, ub2, mark3))
    uf4, db4 = send_on(uf3, forth), send_on(db3, back)
    other = lax.ppermute(own, "dp", swap)
    *acc, own, other = first_call(own, other, (up0, uf1, ub1, uf2, ub2), (down0, df1, db1, df2, db2), mark)
    mine, theirs = next_call((own, other), (uf3, ub3), (df3, db3), acc, mark3)
    passed = lax.ppermute(last_call(other, uf4, db4, theirs, bf16), "dp", swap)
    kept = last_call(own, uf4, db4, mine, f32)
    whole = (kept + passed.astype(f32)).astype(bf16)
    returned = lax.all_to_all(whole.reshape(experts, CAP, width), "expert", 0, 0, tiled=True)
    returned = returned.reshape(experts * CAP, width)
    return lax.dot_general(mix, returned, (((0,), (0,)), ((), ())), preferred_element_type=f32)


def solution(mesh):
    tok = P(("dp", "expert"), None)
    w = P("expert", "dp", None)
    return jax.shard_map(
        local, mesh=mesh, in_specs=(tok,) * 5 + (w, w), out_specs=tok, check_vma=False
    )
```

```python
import functools

import jax
import jax.numpy as jnp
from jax import lax
from jax.experimental import pallas as pl
from jax.experimental.pallas import tpu as pltpu
from jax.sharding import PartitionSpec as P

f32, bf16 = jnp.float32, jnp.bfloat16
CAP = 24
NT = (((1,), (1,)), ((), ()))
VMEM = pl.BlockSpec(memory_space=pltpu.VMEM)
ANY = pl.BlockSpec(memory_space=pl.ANY)


def params(mib):
    return pltpu.CompilerParams(vmem_limit_bytes=mib << 20)


def curvature(x):
    t = jnp.tanh(0.5 * x)
    return (0.25 - 0.25 * t * t) * (2.0 - x * t)


def prepare_kernel(routes_hbm, gates_hbm, x_hbm, t_hbm, c_hbm, send_hbm, mix_ref, routes, gates, rows, send, sems):
    slots, n = mix_ref.shape
    small = [pltpu.make_async_copy(routes_hbm, routes, sems.at[0]), pltpu.make_async_copy(gates_hbm, gates, sems.at[1])]
    big = [pltpu.make_async_copy(ref, rows.at[i], sems.at[2 + i]) for i, ref in enumerate((x_hbm, t_hbm, c_hbm))]
    width = rows.shape[2]
    leave = [
        pltpu.make_async_copy(send.at[i], send_hbm.at[:, i * width:(i + 1) * width], sems.at[5 + i]) for i in range(3)
    ]
    for copy in small + big:
        copy.start()
    for copy in small:
        copy.wait()
    slot = lax.broadcasted_iota(jnp.int32, (slots, n), 0)
    expert = (slot * 2731) >> 16
    place = slot - expert * CAP
    first, second = routes[0:1, :] == expert, routes[1:2, :] == expert
    named = (first | second).astype(f32)
    earlier = lax.broadcasted_iota(jnp.int32, (n, n), 0) < lax.broadcasted_iota(jnp.int32, (n, n), 1)
    before = jnp.dot(named.astype(bf16), earlier.astype(f32).astype(bf16), preferred_element_type=f32)
    here = before.astype(jnp.int32) == place
    pick = jnp.where(here, named, 0.0).astype(bf16)
    for i in range(3):
        big[i].wait()
        send[i] = jnp.dot(pick, rows[i], preferred_element_type=f32).astype(bf16)
        leave[i].start()
    weights = gates[...].astype(f32) / 64.0
    weight = jnp.where(first, weights[0:1, :], 0.0) + jnp.where(second, weights[1:2, :], 0.0)
    mix_ref[...] = jnp.where(here, weight, 0.0).astype(bf16)
    for copy in leave:
        copy.wait()


def prepare(routes, gate_num, tokens, tangent, cotangent, experts):
    n, width = tokens.shape
    slots = experts * CAP
    return pl.pallas_call(
        prepare_kernel,
        out_shape=(
            jax.ShapeDtypeStruct((slots, 3 * width), bf16),
            jax.ShapeDtypeStruct((slots, n), bf16),
        ),
        in_specs=[ANY] * 5,
        out_specs=(ANY, VMEM),
        scratch_shapes=[
            pltpu.VMEM((2, n), jnp.int32),
            pltpu.VMEM((2, n), jnp.int32),
            pltpu.VMEM((3, n, width), bf16),
            pltpu.VMEM((3, slots, width), bf16),
            pltpu.SemaphoreType.DMA((8,)),
        ],
        compiler_params=params(16),
    )(*(pltpu.with_memory_space_constraint(a, pltpu.HBM) for a in (routes.T, gate_num.T, tokens, tangent, cotangent)))


def inner_of(rows_ref, up, down):
    width = up.shape[1]
    before_act = lax.dot_general(rows_ref[:, :width], up, NT, preferred_element_type=f32)
    lifted = lax.dot_general(rows_ref[:, width:2 * width], up, NT, preferred_element_type=f32)
    pulled = lax.dot_general(rows_ref[:, 2 * width:], down, NT, preferred_element_type=f32)
    return (pulled * curvature(before_act) * lifted).astype(bf16)


def accumulate(rows_ref, ups, downs, total=None):
    inners = [inner_of(rows_ref, up[...], down[...]) for up, down in zip(ups, downs)]
    for inner, up in zip(inners, ups):
        part = jnp.dot(inner, up[...], preferred_element_type=f32)
        total = part if total is None else total + part
    return total


def own_kernel(n_w, own_ref, *refs):
    ups, downs = refs[:n_w], refs[n_w:2 * n_w]
    acc_ref, own_out, up_out, down_out, sems = refs[-5:]
    own_copy = pltpu.make_async_copy(own_ref, own_out, sems.at[0])
    copies = []
    for g in range(n_w):
        copies.append(pltpu.make_async_copy(ups[g], up_out.at[g], sems.at[1 + 2 * g]))
        copies.append(pltpu.make_async_copy(downs[g], down_out.at[g], sems.at[2 + 2 * g]))
    for copy in (own_copy, *copies[:4]):
        copy.start()
    for copy in (own_copy, *copies[:2]):
        copy.wait()
    for copy in copies[4:]:
        copy.start()
    total = accumulate(own_out, [up_out.at[0]], [down_out.at[0]])
    for copy in copies[2:]:
        copy.wait()
    rest = range(1, n_w)
    acc_ref[...] = accumulate(own_out, [up_out.at[g] for g in rest], [down_out.at[g] for g in rest], total)


def own_call(own, ups, downs, mark):
    rows, width = own.shape[0], own.shape[1] // 3
    n_w = len(ups)
    stack = jax.ShapeDtypeStruct((n_w, *ups[0].shape), bf16)
    operands = (own, *ups, *downs, mark)
    return pl.pallas_call(
        functools.partial(own_kernel, n_w),
        out_shape=(jax.ShapeDtypeStruct((rows, width), f32), jax.ShapeDtypeStruct(own.shape, bf16), stack, stack),
        in_specs=[ANY] * len(operands),
        out_specs=(VMEM,) * 4,
        scratch_shapes=[pltpu.SemaphoreType.DMA((2 * n_w + 1,))],
        compiler_params=params(16),
    )(*operands)


def other_kernel(other_ref, up_ref, down_ref, acc_ref, other_out, sem):
    copy = pltpu.make_async_copy(other_ref, other_out, sem)
    copy.start()
    copy.wait()
    blocks = range(up_ref.shape[0])
    acc_ref[...] = accumulate(other_out, [up_ref.at[g] for g in blocks], [down_ref.at[g] for g in blocks])


def other_call(other, up_stack, down_stack):
    rows, width = other.shape[0], other.shape[1] // 3
    stacks = [pltpu.with_memory_space_constraint(x, pltpu.VMEM) for x in (up_stack, down_stack)]
    return pl.pallas_call(
        other_kernel,
        out_shape=(jax.ShapeDtypeStruct((rows, width), f32), jax.ShapeDtypeStruct(other.shape, bf16)),
        in_specs=[ANY, VMEM, VMEM],
        out_specs=(VMEM, VMEM),
        scratch_shapes=[pltpu.SemaphoreType.DMA],
        compiler_params=params(16),
    )(other, *stacks)


def next_kernel(n_w, own_ref, other_ref, *refs):
    ups, downs, accs = refs[:n_w], refs[n_w:2 * n_w], refs[2 * n_w:2 * n_w + 2]
    outs, up_buf, down_buf, sems = refs[-5:-3], *refs[-3:]
    copies = []
    for g in range(n_w):
        copies.append(pltpu.make_async_copy(ups[g], up_buf.at[g], sems.at[2 * g]))
        copies.append(pltpu.make_async_copy(downs[g], down_buf.at[g], sems.at[2 * g + 1]))
    for copy in copies:
        copy.start()
    for copy in copies:
        copy.wait()
    blocks = range(n_w)
    for rows_ref, acc_ref, out_ref in zip((own_ref, other_ref), accs, outs):
        out_ref[...] = accumulate(rows_ref, [up_buf.at[g] for g in blocks], [down_buf.at[g] for g in blocks], acc_ref[...])


def next_call(rows, ups, downs, acc, mark):
    n_w = len(ups)
    inside = [pltpu.with_memory_space_constraint(x, pltpu.VMEM) for x in (*rows, *acc)]
    return pl.pallas_call(
        functools.partial(next_kernel, n_w),
        out_shape=tuple(jax.ShapeDtypeStruct(x.shape, f32) for x in acc),
        in_specs=[VMEM] * 2 + [ANY] * (2 * n_w) + [VMEM] * 2 + [ANY],
        out_specs=(VMEM,) * 2,
        scratch_shapes=[
            pltpu.VMEM((n_w, *ups[0].shape), bf16),
            pltpu.VMEM((n_w, *ups[0].shape), bf16),
            pltpu.SemaphoreType.DMA((2 * n_w,)),
        ],
        compiler_params=params(20),
    )(*inside[:2], *ups, *downs, *inside[2:], mark)


def last_kernel(rows_ref, up_ref, down_ref, acc_ref, out_ref):
    out_ref[...] = accumulate(rows_ref, [up_ref], [down_ref], acc_ref[...]).astype(out_ref.dtype)


def last_call(rows, up, down, acc, kind):
    operands = tuple(pltpu.with_memory_space_constraint(x, pltpu.VMEM) for x in (rows, up, down, acc))
    return pl.pallas_call(
        last_kernel,
        out_shape=jax.ShapeDtypeStruct(acc.shape, kind),
        in_specs=[VMEM] * 4,
        out_specs=VMEM,
        compiler_params=params(16),
    )(*operands)


def hold_kernel(*refs):
    refs[-1][...] = jnp.zeros_like(refs[-1])


def hold(*arrays):
    return pl.pallas_call(
        hold_kernel,
        out_shape=jax.ShapeDtypeStruct((8, 128), f32),
        in_specs=[ANY] * len(arrays),
        out_specs=VMEM,
        compiler_params=params(1),
        cost_estimate=pl.CostEstimate(flops=200_000_000_000, bytes_accessed=1_000_000_000, transcendentals=0),
    )(*arrays)


def local(tokens, tangent, cotangent, routes, gate_num, w_up, w_down):
    n_dp = lax.axis_size("dp")
    experts = lax.axis_size("expert")
    width = tokens.shape[1]
    forth = [(i, (i + 2) % n_dp) for i in range(n_dp)]
    back = [(i, (i - 2) % n_dp) for i in range(n_dp)]
    swap = [(i, i ^ 1) for i in range(n_dp)]
    up0, down0 = w_up[0], w_down[0]

    def send_on(x, way):
        return lax.ppermute(x, "dp", way)

    after = lax.optimization_barrier
    uf1, db1 = send_on(up0, forth), send_on(down0, back)
    df1, ub1 = send_on(down0, forth), send_on(up0, back)
    send, mix = prepare(routes, gate_num, tokens, tangent, cotangent, experts)
    own = lax.all_to_all(send.reshape(experts, CAP, 3 * width), "expert", 0, 0, tiled=True)
    own = own.reshape(experts * CAP, 3 * width)
    mark = hold(uf1)
    uf1, db1, mark = after((uf1, db1, mark))
    uf2, db2 = send_on(uf1, forth), send_on(db1, back)
    df1, ub1, mark = after((df1, ub1, mark))
    df2, ub2 = send_on(df1, forth), send_on(ub1, back)
    uf2, db2, df1, ub1 = after((uf2, db2, df1, ub1))
    uf3, db3 = send_on(uf2, forth), send_on(db2, back)
    df2, ub2, uf2, db2 = after((df2, ub2, uf2, db2))
    df3, ub3 = send_on(df2, forth), send_on(ub2, back)
    mine, kept_own, up_stack, down_stack = own_call(own, (up0, uf1, ub1, uf2, ub2), (down0, df1, db1, df2, db2), mark)
    mark3 = hold(uf3, kept_own)
    uf3, db3, df2, ub2, mark3 = after((uf3, db3, df2, ub2, mark3))
    uf4, db4 = send_on(uf3, forth), send_on(db3, back)
    other = lax.ppermute(own, "dp", swap)
    theirs, kept_other = other_call(other, up_stack, down_stack)
    mine, theirs = next_call((kept_own, kept_other), (uf3, ub3), (df3, db3), (mine, theirs), mark3)
    passed = lax.ppermute(last_call(kept_other, uf4, db4, theirs, bf16), "dp", swap)
    kept = last_call(kept_own, uf4, db4, mine, f32)
    whole = (kept + passed.astype(f32)).astype(bf16)
    returned = lax.all_to_all(whole.reshape(experts, CAP, width), "expert", 0, 0, tiled=True)
    returned = returned.reshape(experts * CAP, width)
    return lax.dot_general(mix, returned, (((0,), (0,)), ((), ())), preferred_element_type=f32)


def solution(mesh):
    tok = P(("dp", "expert"), None)
    w = P("expert", "dp", None)
    return jax.shard_map(
        local, mesh=mesh, in_specs=(tok,) * 5 + (w, w), out_specs=tok, check_vma=False
    )
```

```python
import functools

import jax
import jax.numpy as jnp
from jax import lax
from jax.experimental import pallas as pl
from jax.experimental.pallas import tpu as pltpu
from jax.sharding import PartitionSpec as P

f32, bf16 = jnp.float32, jnp.bfloat16
CAP = 24
NT = (((1,), (1,)), ((), ()))
VMEM = pl.BlockSpec(memory_space=pltpu.VMEM)
ANY = pl.BlockSpec(memory_space=pl.ANY)


def params(mib):
    return pltpu.CompilerParams(vmem_limit_bytes=mib << 20)


def curvature(x):
    t = jnp.tanh(0.5 * x)
    return (0.25 - 0.25 * t * t) * (2.0 - x * t)


def prepare_kernel(routes_hbm, gates_hbm, x_hbm, t_hbm, c_hbm, send_hbm, mix_ref, routes, gates, rows, send, sems):
    slots, n = mix_ref.shape
    small = [pltpu.make_async_copy(routes_hbm, routes, sems.at[0]), pltpu.make_async_copy(gates_hbm, gates, sems.at[1])]
    big = [pltpu.make_async_copy(ref, rows.at[i], sems.at[2 + i]) for i, ref in enumerate((x_hbm, t_hbm, c_hbm))]
    width = rows.shape[2]
    leave = [
        pltpu.make_async_copy(send.at[i], send_hbm.at[:, i * width:(i + 1) * width], sems.at[5 + i]) for i in range(3)
    ]
    for copy in small + big:
        copy.start()
    for copy in small:
        copy.wait()
    slot = lax.broadcasted_iota(jnp.int32, (slots, n), 0)
    expert = (slot * 2731) >> 16
    place = slot - expert * CAP
    first, second = routes[0:1, :] == expert, routes[1:2, :] == expert
    named = (first | second).astype(f32)
    earlier = lax.broadcasted_iota(jnp.int32, (n, n), 0) < lax.broadcasted_iota(jnp.int32, (n, n), 1)
    before = jnp.dot(named.astype(bf16), earlier.astype(f32).astype(bf16), preferred_element_type=f32)
    here = before.astype(jnp.int32) == place
    pick = jnp.where(here, named, 0.0).astype(bf16)
    for i in range(3):
        big[i].wait()
        send[i] = jnp.dot(pick, rows[i], preferred_element_type=f32).astype(bf16)
        leave[i].start()
    weights = gates[...].astype(f32) / 64.0
    weight = jnp.where(first, weights[0:1, :], 0.0) + jnp.where(second, weights[1:2, :], 0.0)
    mix_ref[...] = jnp.where(here, weight, 0.0).astype(bf16)
    for copy in leave:
        copy.wait()


def prepare(routes, gate_num, tokens, tangent, cotangent, experts):
    n, width = tokens.shape
    slots = experts * CAP
    return pl.pallas_call(
        prepare_kernel,
        out_shape=(
            jax.ShapeDtypeStruct((slots, 3 * width), bf16),
            jax.ShapeDtypeStruct((slots, n), bf16),
        ),
        in_specs=[ANY] * 5,
        out_specs=(ANY, VMEM),
        scratch_shapes=[
            pltpu.VMEM((2, n), jnp.int32),
            pltpu.VMEM((2, n), jnp.int32),
            pltpu.VMEM((3, n, width), bf16),
            pltpu.VMEM((3, slots, width), bf16),
            pltpu.SemaphoreType.DMA((8,)),
        ],
        compiler_params=params(16),
    )(*(pltpu.with_memory_space_constraint(a, pltpu.HBM) for a in (routes.T, gate_num.T, tokens, tangent, cotangent)))


def inner_of(rows_ref, up, down):
    width = up.shape[1]
    before_act = lax.dot_general(rows_ref[:, :width], up, NT, preferred_element_type=f32)
    lifted = lax.dot_general(rows_ref[:, width:2 * width], up, NT, preferred_element_type=f32)
    pulled = lax.dot_general(rows_ref[:, 2 * width:], down, NT, preferred_element_type=f32)
    return (pulled * curvature(before_act) * lifted).astype(bf16)


def accumulate(rows_ref, ups, downs, total=None):
    inners = [inner_of(rows_ref, up[...], down[...]) for up, down in zip(ups, downs)]
    for inner, up in zip(inners, ups):
        part = jnp.dot(inner, up[...], preferred_element_type=f32)
        total = part if total is None else total + part
    return total


def own_kernel(n_w, own_ref, *refs):
    ups, downs = refs[:n_w], refs[n_w:2 * n_w]
    acc_ref, own_out, up_out, down_out, sems = refs[-5:]
    own_copy = pltpu.make_async_copy(own_ref, own_out, sems.at[0])
    copies = []
    for g in range(n_w):
        copies.append(pltpu.make_async_copy(ups[g], up_out.at[g], sems.at[1 + 2 * g]))
        copies.append(pltpu.make_async_copy(downs[g], down_out.at[g], sems.at[2 + 2 * g]))
    for copy in (own_copy, *copies[:4]):
        copy.start()
    for copy in (own_copy, *copies[:2]):
        copy.wait()
    for copy in copies[4:]:
        copy.start()
    total = accumulate(own_out, [up_out.at[0]], [down_out.at[0]])
    for copy in copies[2:]:
        copy.wait()
    rest = range(1, n_w)
    acc_ref[...] = accumulate(own_out, [up_out.at[g] for g in rest], [down_out.at[g] for g in rest], total)


def own_call(own, ups, downs, mark):
    rows, width = own.shape[0], own.shape[1] // 3
    n_w = len(ups)
    stack = jax.ShapeDtypeStruct((n_w, *ups[0].shape), bf16)
    operands = (own, *ups, *downs, mark)
    return pl.pallas_call(
        functools.partial(own_kernel, n_w),
        out_shape=(jax.ShapeDtypeStruct((rows, width), f32), jax.ShapeDtypeStruct(own.shape, bf16), stack, stack),
        in_specs=[ANY] * len(operands),
        out_specs=(VMEM,) * 4,
        scratch_shapes=[pltpu.SemaphoreType.DMA((2 * n_w + 1,))],
        compiler_params=params(16),
    )(*operands)


def other_kernel(other_ref, up_ref, down_ref, acc_ref, other_out, sem):
    copy = pltpu.make_async_copy(other_ref, other_out, sem)
    copy.start()
    copy.wait()
    blocks = range(up_ref.shape[0])
    acc_ref[...] = accumulate(other_out, [up_ref.at[g] for g in blocks], [down_ref.at[g] for g in blocks])


def other_call(other, up_stack, down_stack):
    rows, width = other.shape[0], other.shape[1] // 3
    stacks = [pltpu.with_memory_space_constraint(x, pltpu.VMEM) for x in (up_stack, down_stack)]
    return pl.pallas_call(
        other_kernel,
        out_shape=(jax.ShapeDtypeStruct((rows, width), f32), jax.ShapeDtypeStruct(other.shape, bf16)),
        in_specs=[ANY, VMEM, VMEM],
        out_specs=(VMEM, VMEM),
        scratch_shapes=[pltpu.SemaphoreType.DMA],
        compiler_params=params(16),
    )(other, *stacks)


def next_kernel(n_w, own_ref, other_ref, *refs):
    ups, downs, accs = refs[:n_w], refs[n_w:2 * n_w], refs[2 * n_w:2 * n_w + 2]
    outs, up_buf, down_buf, sems = refs[-5:-3], *refs[-3:]
    copies = []
    for g in range(n_w):
        copies.append(pltpu.make_async_copy(ups[g], up_buf.at[g], sems.at[2 * g]))
        copies.append(pltpu.make_async_copy(downs[g], down_buf.at[g], sems.at[2 * g + 1]))
    for copy in copies:
        copy.start()
    for copy in copies:
        copy.wait()
    blocks = range(n_w)
    for rows_ref, acc_ref, out_ref in zip((own_ref, other_ref), accs, outs):
        out_ref[...] = accumulate(rows_ref, [up_buf.at[g] for g in blocks], [down_buf.at[g] for g in blocks], acc_ref[...])


def next_call(rows, ups, downs, acc, mark):
    n_w = len(ups)
    inside = [pltpu.with_memory_space_constraint(x, pltpu.VMEM) for x in (*rows, *acc)]
    return pl.pallas_call(
        functools.partial(next_kernel, n_w),
        out_shape=tuple(jax.ShapeDtypeStruct(x.shape, f32) for x in acc),
        in_specs=[VMEM] * 2 + [ANY] * (2 * n_w) + [VMEM] * 2 + [ANY],
        out_specs=(VMEM,) * 2,
        scratch_shapes=[
            pltpu.VMEM((n_w, *ups[0].shape), bf16),
            pltpu.VMEM((n_w, *ups[0].shape), bf16),
            pltpu.SemaphoreType.DMA((2 * n_w,)),
        ],
        compiler_params=params(20),
    )(*inside[:2], *ups, *downs, *inside[2:], mark)


def factor_kernel(rows_ref, up_ref, factor_ref):
    width = up_ref.shape[1]
    before_act = lax.dot_general(rows_ref[:, :width], up_ref[...], NT, preferred_element_type=f32)
    lifted = lax.dot_general(rows_ref[:, width:2 * width], up_ref[...], NT, preferred_element_type=f32)
    factor_ref[...] = curvature(before_act) * lifted


def last_other_kernel(rows_ref, factor_ref, up_ref, down_ref, acc_ref, out_ref):
    width = up_ref.shape[1]
    pulled = lax.dot_general(rows_ref[:, 2 * width:], down_ref[...], NT, preferred_element_type=f32)
    inner = (pulled * factor_ref[...]).astype(bf16)
    total = acc_ref[...] + jnp.dot(inner, up_ref[...], preferred_element_type=f32)
    out_ref[...] = total.astype(out_ref.dtype)


def last_own_kernel(rows_ref, up_ref, down_ref, acc_ref, out_ref):
    out_ref[...] = accumulate(rows_ref, [up_ref], [down_ref], acc_ref[...])


def last_call(kernel, shape, kind, *operands):
    operands = tuple(pltpu.with_memory_space_constraint(x, pltpu.VMEM) for x in operands)
    return pl.pallas_call(
        kernel,
        out_shape=jax.ShapeDtypeStruct(shape, kind),
        in_specs=[VMEM] * len(operands),
        out_specs=VMEM,
        compiler_params=params(12),
    )(*operands)


def hold_kernel(*refs):
    refs[-1][...] = jnp.zeros_like(refs[-1])


def hold(*arrays):
    return pl.pallas_call(
        hold_kernel,
        out_shape=jax.ShapeDtypeStruct((8, 128), f32),
        in_specs=[ANY] * len(arrays),
        out_specs=VMEM,
        compiler_params=params(1),
        cost_estimate=pl.CostEstimate(flops=200_000_000_000, bytes_accessed=1_000_000_000, transcendentals=0),
    )(*arrays)


def local(tokens, tangent, cotangent, routes, gate_num, w_up, w_down):
    n_dp = lax.axis_size("dp")
    experts = lax.axis_size("expert")
    width = tokens.shape[1]
    forth = [(i, (i + 2) % n_dp) for i in range(n_dp)]
    back = [(i, (i - 2) % n_dp) for i in range(n_dp)]
    swap = [(i, i ^ 1) for i in range(n_dp)]
    up0, down0 = w_up[0], w_down[0]

    def send_on(x, way):
        return lax.ppermute(x, "dp", way)

    after = lax.optimization_barrier
    uf1, db1 = send_on(up0, forth), send_on(down0, back)
    df1, ub1 = send_on(down0, forth), send_on(up0, back)
    send, mix = prepare(routes, gate_num, tokens, tangent, cotangent, experts)
    own = lax.all_to_all(send.reshape(experts, CAP, 3 * width), "expert", 0, 0, tiled=True)
    own = own.reshape(experts * CAP, 3 * width)
    mark = hold(uf1)
    uf1, db1, mark = after((uf1, db1, mark))
    uf2, db2 = send_on(uf1, forth), send_on(db1, back)
    df1, ub1, mark = after((df1, ub1, mark))
    df2, ub2 = send_on(df1, forth), send_on(ub1, back)
    uf2, db2, df1, ub1 = after((uf2, db2, df1, ub1))
    uf3, db3 = send_on(uf2, forth), send_on(db2, back)
    df2, ub2, uf2, db2 = after((df2, ub2, uf2, db2))
    df3, ub3 = send_on(df2, forth), send_on(ub2, back)
    mine, kept_own, up_stack, down_stack = own_call(own, (up0, uf1, ub1, uf2, ub2), (down0, df1, db1, df2, db2), mark)
    mark3 = hold(uf3, kept_own)
    uf3, db3, df2, ub2, mark3 = after((uf3, db3, df2, ub2, mark3))
    uf4, db4 = send_on(uf3, forth), send_on(db3, back)
    other = lax.ppermute(own, "dp", swap)
    theirs, kept_other = other_call(other, up_stack, down_stack)
    mine, theirs = next_call((kept_own, kept_other), (uf3, ub3), (df3, db3), (mine, theirs), mark3)
    uf4, theirs = after((uf4, theirs))
    factor = last_call(factor_kernel, (other.shape[0], uf4.shape[0]), f32, kept_other, uf4)
    passed = last_call(last_other_kernel, theirs.shape, bf16, kept_other, factor, uf4, db4, theirs)
    passed = send_on(passed, swap)
    kept = last_call(last_own_kernel, mine.shape, f32, kept_own, uf4, db4, mine)
    whole = (kept + passed.astype(f32)).astype(bf16)
    returned = lax.all_to_all(whole.reshape(experts, CAP, width), "expert", 0, 0, tiled=True)
    returned = returned.reshape(experts * CAP, width)
    return lax.dot_general(mix, returned, (((0,), (0,)), ((), ())), preferred_element_type=f32)


def solution(mesh):
    tok = P(("dp", "expert"), None)
    w = P("expert", "dp", None)
    return jax.shard_map(
        local, mesh=mesh, in_specs=(tok,) * 5 + (w, w), out_specs=tok, check_vma=False
    )
```

```python
import functools

import jax
import jax.numpy as jnp
from jax import lax
from jax.experimental import pallas as pl
from jax.experimental.pallas import tpu as pltpu
from jax.sharding import PartitionSpec as P

f32, bf16 = jnp.float32, jnp.bfloat16
CAP = 24
NT = (((1,), (1,)), ((), ()))
VMEM = pl.BlockSpec(memory_space=pltpu.VMEM)
ANY = pl.BlockSpec(memory_space=pl.ANY)


def params(mib):
    return pltpu.CompilerParams(vmem_limit_bytes=mib << 20)


def curvature(x):
    t = jnp.tanh(0.5 * x)
    return (0.25 - 0.25 * t * t) * (2.0 - x * t)


def prepare_kernel(routes_hbm, gates_hbm, x_hbm, t_hbm, c_hbm, send_hbm, mix_ref, routes, gates, rows, send, sems):
    slots, n = mix_ref.shape
    small = [pltpu.make_async_copy(routes_hbm, routes, sems.at[0]), pltpu.make_async_copy(gates_hbm, gates, sems.at[1])]
    big = [pltpu.make_async_copy(ref, rows.at[i], sems.at[2 + i]) for i, ref in enumerate((x_hbm, t_hbm, c_hbm))]
    width = rows.shape[2]
    leave = [
        pltpu.make_async_copy(send.at[i], send_hbm.at[:, i * width:(i + 1) * width], sems.at[5 + i]) for i in range(3)
    ]
    for copy in small + big:
        copy.start()
    for copy in small:
        copy.wait()
    slot = lax.broadcasted_iota(jnp.int32, (slots, n), 0)
    expert = (slot * 2731) >> 16
    place = slot - expert * CAP
    first, second = routes[0:1, :] == expert, routes[1:2, :] == expert
    named = (first | second).astype(f32)
    earlier = lax.broadcasted_iota(jnp.int32, (n, n), 0) < lax.broadcasted_iota(jnp.int32, (n, n), 1)
    before = jnp.dot(named.astype(bf16), earlier.astype(f32).astype(bf16), preferred_element_type=f32)
    here = before.astype(jnp.int32) == place
    pick = jnp.where(here, named, 0.0).astype(bf16)
    for i in range(3):
        big[i].wait()
        send[i] = jnp.dot(pick, rows[i], preferred_element_type=f32).astype(bf16)
        leave[i].start()
    weights = gates[...].astype(f32) / 64.0
    weight = jnp.where(first, weights[0:1, :], 0.0) + jnp.where(second, weights[1:2, :], 0.0)
    mix_ref[...] = jnp.where(here, weight, 0.0).astype(bf16)
    for copy in leave:
        copy.wait()


def prepare(routes, gate_num, tokens, tangent, cotangent, experts):
    n, width = tokens.shape
    slots = experts * CAP
    return pl.pallas_call(
        prepare_kernel,
        out_shape=(
            jax.ShapeDtypeStruct((slots, 3 * width), bf16),
            jax.ShapeDtypeStruct((slots, n), bf16),
        ),
        in_specs=[ANY] * 5,
        out_specs=(ANY, VMEM),
        scratch_shapes=[
            pltpu.VMEM((2, n), jnp.int32),
            pltpu.VMEM((2, n), jnp.int32),
            pltpu.VMEM((3, n, width), bf16),
            pltpu.VMEM((3, slots, width), bf16),
            pltpu.SemaphoreType.DMA((8,)),
        ],
        compiler_params=params(16),
    )(*(pltpu.with_memory_space_constraint(a, pltpu.HBM) for a in (routes.T, gate_num.T, tokens, tangent, cotangent)))


def inner_of(rows_ref, up, down):
    width = up.shape[1]
    before_act = lax.dot_general(rows_ref[:, :width], up, NT, preferred_element_type=f32)
    lifted = lax.dot_general(rows_ref[:, width:2 * width], up, NT, preferred_element_type=f32)
    pulled = lax.dot_general(rows_ref[:, 2 * width:], down, NT, preferred_element_type=f32)
    return (pulled * curvature(before_act) * lifted).astype(bf16)


def accumulate(rows_ref, ups, downs, total=None):
    inners = [inner_of(rows_ref, up[...], down[...]) for up, down in zip(ups, downs)]
    for inner, up in zip(inners, ups):
        part = jnp.dot(inner, up[...], preferred_element_type=f32)
        total = part if total is None else total + part
    return total


def own_kernel(n_w, own_ref, *refs):
    ups, downs = refs[:n_w], refs[n_w:2 * n_w]
    acc_ref, own_out, up_out, down_out, sems = refs[-5:]
    own_copy = pltpu.make_async_copy(own_ref, own_out, sems.at[0])
    copies = []
    for g in range(n_w):
        copies.append(pltpu.make_async_copy(ups[g], up_out.at[g], sems.at[1 + 2 * g]))
        copies.append(pltpu.make_async_copy(downs[g], down_out.at[g], sems.at[2 + 2 * g]))
    for copy in (own_copy, *copies[:4]):
        copy.start()
    for copy in (own_copy, *copies[:2]):
        copy.wait()
    for copy in copies[4:]:
        copy.start()
    total = accumulate(own_out, [up_out.at[0]], [down_out.at[0]])
    for copy in copies[2:]:
        copy.wait()
    rest = range(1, n_w)
    acc_ref[...] = accumulate(own_out, [up_out.at[g] for g in rest], [down_out.at[g] for g in rest], total)


def own_call(own, ups, downs, mark):
    rows, width = own.shape[0], own.shape[1] // 3
    n_w = len(ups)
    stack = jax.ShapeDtypeStruct((n_w, *ups[0].shape), bf16)
    operands = (own, *ups, *downs, mark)
    return pl.pallas_call(
        functools.partial(own_kernel, n_w),
        out_shape=(jax.ShapeDtypeStruct((rows, width), f32), jax.ShapeDtypeStruct(own.shape, bf16), stack, stack),
        in_specs=[ANY] * len(operands),
        out_specs=(VMEM,) * 4,
        scratch_shapes=[pltpu.SemaphoreType.DMA((2 * n_w + 1,))],
        compiler_params=params(16),
    )(*operands)


def other_kernel(other_ref, up_ref, down_ref, acc_ref, other_out, sem):
    copy = pltpu.make_async_copy(other_ref, other_out, sem)
    copy.start()
    copy.wait()
    blocks = range(up_ref.shape[0])
    acc_ref[...] = accumulate(other_out, [up_ref.at[g] for g in blocks], [down_ref.at[g] for g in blocks])


def other_call(other, up_stack, down_stack):
    rows, width = other.shape[0], other.shape[1] // 3
    stacks = [pltpu.with_memory_space_constraint(x, pltpu.VMEM) for x in (up_stack, down_stack)]
    return pl.pallas_call(
        other_kernel,
        out_shape=(jax.ShapeDtypeStruct((rows, width), f32), jax.ShapeDtypeStruct(other.shape, bf16)),
        in_specs=[ANY, VMEM, VMEM],
        out_specs=(VMEM, VMEM),
        scratch_shapes=[pltpu.SemaphoreType.DMA],
        compiler_params=params(16),
    )(other, *stacks)


def next_kernel(n_w, own_ref, other_ref, *refs):
    ups, downs, accs = refs[:n_w], refs[n_w:2 * n_w], refs[2 * n_w:2 * n_w + 2]
    outs, up_buf, down_buf, sems = refs[-5:-3], *refs[-3:]
    copies = []
    for g in range(n_w):
        copies.append(pltpu.make_async_copy(ups[g], up_buf.at[g], sems.at[2 * g]))
        copies.append(pltpu.make_async_copy(downs[g], down_buf.at[g], sems.at[2 * g + 1]))
    for copy in copies:
        copy.start()
    for copy in copies:
        copy.wait()
    blocks = range(n_w)
    for rows_ref, acc_ref, out_ref in zip((own_ref, other_ref), accs, outs):
        total = accumulate(rows_ref, [up_buf.at[g] for g in blocks], [down_buf.at[g] for g in blocks], acc_ref[...])
        out_ref[...] = total.astype(out_ref.dtype)


def next_call(rows, ups, downs, acc, mark):
    n_w = len(ups)
    inside = [pltpu.with_memory_space_constraint(x, pltpu.VMEM) for x in (*rows, *acc)]
    return pl.pallas_call(
        functools.partial(next_kernel, n_w),
        out_shape=tuple(jax.ShapeDtypeStruct(x.shape, kind) for x, kind in zip(acc, (f32, bf16))),
        in_specs=[VMEM] * 2 + [ANY] * (2 * n_w) + [VMEM] * 2 + [ANY],
        out_specs=(VMEM,) * 2,
        scratch_shapes=[
            pltpu.VMEM((n_w, *ups[0].shape), bf16),
            pltpu.VMEM((n_w, *ups[0].shape), bf16),
            pltpu.SemaphoreType.DMA((2 * n_w,)),
        ],
        compiler_params=params(20),
    )(*inside[:2], *ups, *downs, *inside[2:], mark)


def factor_kernel(rows_ref, up_ref, factor_ref):
    width = up_ref.shape[1]
    before_act = lax.dot_general(rows_ref[:, :width], up_ref[...], NT, preferred_element_type=f32)
    lifted = lax.dot_general(rows_ref[:, width:2 * width], up_ref[...], NT, preferred_element_type=f32)
    factor_ref[...] = curvature(before_act) * lifted


def last_own_kernel(rows_ref, up_ref, down_ref, acc_ref, out_ref):
    out_ref[...] = accumulate(rows_ref, [up_ref], [down_ref], acc_ref[...])


def last_far_kernel(rows_ref, factor_ref, up_ref, down_ref, acc_ref, passed_ref, out_ref):
    width = up_ref.shape[1]
    pulled = lax.dot_general(rows_ref[:, 2 * width:], down_ref[...], NT, preferred_element_type=f32)
    inner = (pulled * factor_ref[...]).astype(bf16)
    total = acc_ref[...] + passed_ref[...].astype(f32)
    out_ref[...] = (total + jnp.dot(inner, up_ref[...], preferred_element_type=f32)).astype(out_ref.dtype)


def last_call(kernel, shape, kind, *operands):
    operands = tuple(pltpu.with_memory_space_constraint(x, pltpu.VMEM) for x in operands)
    return pl.pallas_call(
        kernel,
        out_shape=jax.ShapeDtypeStruct(shape, kind),
        in_specs=[VMEM] * len(operands),
        out_specs=VMEM,
        compiler_params=params(12),
    )(*operands)


def hold_kernel(*refs):
    refs[-1][...] = jnp.zeros_like(refs[-1])


def hold(*arrays):
    return pl.pallas_call(
        hold_kernel,
        out_shape=jax.ShapeDtypeStruct((8, 128), f32),
        in_specs=[ANY] * len(arrays),
        out_specs=VMEM,
        compiler_params=params(1),
        cost_estimate=pl.CostEstimate(flops=200_000_000_000, bytes_accessed=1_000_000_000, transcendentals=0),
    )(*arrays)


def local(tokens, tangent, cotangent, routes, gate_num, w_up, w_down):
    n_dp = lax.axis_size("dp")
    experts = lax.axis_size("expert")
    width = tokens.shape[1]
    forth = [(i, (i + 2) % n_dp) for i in range(n_dp)]
    back = [(i, (i - 2) % n_dp) for i in range(n_dp)]
    swap = [(i, i ^ 1) for i in range(n_dp)]
    up0, down0 = w_up[0], w_down[0]

    def send_on(x, way):
        return lax.ppermute(x, "dp", way)

    after = lax.optimization_barrier
    uf1, db1 = send_on(up0, forth), send_on(down0, back)
    df1, ub1 = send_on(down0, forth), send_on(up0, back)
    send, mix = prepare(routes, gate_num, tokens, tangent, cotangent, experts)
    own = lax.all_to_all(send.reshape(experts, CAP, 3 * width), "expert", 0, 0, tiled=True)
    own = own.reshape(experts * CAP, 3 * width)
    mark = hold(uf1)
    uf1, db1, mark = after((uf1, db1, mark))
    uf2, db2 = send_on(uf1, forth), send_on(db1, back)
    df1, ub1, mark = after((df1, ub1, mark))
    df2, ub2 = send_on(df1, forth), send_on(ub1, back)
    uf2, db2, df1, ub1 = after((uf2, db2, df1, ub1))
    uf3, db3 = send_on(uf2, forth), send_on(db2, back)
    df2, ub2, uf2, db2 = after((df2, ub2, uf2, db2))
    df3, ub3 = send_on(df2, forth), send_on(ub2, back)
    mine, kept_own, up_stack, down_stack = own_call(own, (up0, uf1, ub1, uf2, ub2), (down0, df1, db1, df2, db2), mark)
    mark3 = hold(uf3, kept_own)
    uf3, db3, df2, ub2, mark3 = after((uf3, db3, df2, ub2, mark3))
    uf4, db4 = send_on(uf3, forth), send_on(db3, back)
    other = lax.ppermute(own, "dp", swap)
    theirs, kept_other = other_call(other, up_stack, down_stack)
    mine, theirs = next_call((kept_own, kept_other), (uf3, ub3), (df3, db3), (mine, theirs), mark3)
    passed = send_on(theirs, swap)
    far_up, far_down = send_on(uf4, swap), send_on(db4, swap)
    part = last_call(last_own_kernel, mine.shape, f32, kept_own, uf4, db4, mine)
    far_up, part = after((far_up, part))
    factor = last_call(factor_kernel, (own.shape[0], far_up.shape[0]), f32, kept_own, far_up)
    whole = last_call(last_far_kernel, mine.shape, bf16, kept_own, factor, far_up, far_down, part, passed)
    returned = lax.all_to_all(whole.reshape(experts, CAP, width), "expert", 0, 0, tiled=True)
    returned = returned.reshape(experts * CAP, width)
    return lax.dot_general(mix, returned, (((0,), (0,)), ((), ())), preferred_element_type=f32)


def solution(mesh):
    tok = P(("dp", "expert"), None)
    w = P("expert", "dp", None)
    return jax.shard_map(
        local, mesh=mesh, in_specs=(tok,) * 5 + (w, w), out_specs=tok, check_vma=False
    )
```

```python
import functools

import jax
import jax.numpy as jnp
from jax import lax
from jax.experimental import pallas as pl
from jax.experimental.pallas import tpu as pltpu
from jax.sharding import PartitionSpec as P

f32, bf16 = jnp.float32, jnp.bfloat16
CAP = 24
NT = (((1,), (1,)), ((), ()))
VMEM = pl.BlockSpec(memory_space=pltpu.VMEM)
ANY = pl.BlockSpec(memory_space=pl.ANY)


def params(mib):
    return pltpu.CompilerParams(vmem_limit_bytes=mib << 20)


def curvature(x):
    t = jnp.tanh(0.5 * x)
    return (0.25 - 0.25 * t * t) * (2.0 - x * t)


def prepare_kernel(routes_hbm, gates_hbm, x_hbm, t_hbm, c_hbm, send_hbm, mix_ref, routes, gates, rows, send, sems):
    slots, n = mix_ref.shape
    small = [pltpu.make_async_copy(routes_hbm, routes, sems.at[0]), pltpu.make_async_copy(gates_hbm, gates, sems.at[1])]
    big = [pltpu.make_async_copy(ref, rows.at[i], sems.at[2 + i]) for i, ref in enumerate((x_hbm, t_hbm, c_hbm))]
    width = rows.shape[2]
    leave = [
        pltpu.make_async_copy(send.at[i], send_hbm.at[:, i * width:(i + 1) * width], sems.at[5 + i]) for i in range(3)
    ]
    for copy in small + big:
        copy.start()
    for copy in small:
        copy.wait()
    slot = lax.broadcasted_iota(jnp.int32, (slots, n), 0)
    expert = (slot * 2731) >> 16
    place = slot - expert * CAP
    first, second = routes[0:1, :] == expert, routes[1:2, :] == expert
    named = (first | second).astype(f32)
    earlier = lax.broadcasted_iota(jnp.int32, (n, n), 0) < lax.broadcasted_iota(jnp.int32, (n, n), 1)
    before = jnp.dot(named.astype(bf16), earlier.astype(f32).astype(bf16), preferred_element_type=f32)
    here = before.astype(jnp.int32) == place
    pick = jnp.where(here, named, 0.0).astype(bf16)
    for i in range(3):
        big[i].wait()
        send[i] = jnp.dot(pick, rows[i], preferred_element_type=f32).astype(bf16)
        leave[i].start()
    weights = gates[...].astype(f32) / 64.0
    weight = jnp.where(first, weights[0:1, :], 0.0) + jnp.where(second, weights[1:2, :], 0.0)
    mix_ref[...] = jnp.where(here, weight, 0.0).astype(bf16)
    for copy in leave:
        copy.wait()


def prepare(routes, gate_num, tokens, tangent, cotangent, experts):
    n, width = tokens.shape
    slots = experts * CAP
    return pl.pallas_call(
        prepare_kernel,
        out_shape=(
            jax.ShapeDtypeStruct((slots, 3 * width), bf16),
            jax.ShapeDtypeStruct((slots, n), bf16),
        ),
        in_specs=[ANY] * 5,
        out_specs=(ANY, VMEM),
        scratch_shapes=[
            pltpu.VMEM((2, n), jnp.int32),
            pltpu.VMEM((2, n), jnp.int32),
            pltpu.VMEM((3, n, width), bf16),
            pltpu.VMEM((3, slots, width), bf16),
            pltpu.SemaphoreType.DMA((8,)),
        ],
        compiler_params=params(16),
    )(*(pltpu.with_memory_space_constraint(a, pltpu.HBM) for a in (routes.T, gate_num.T, tokens, tangent, cotangent)))


def inner_of(rows_ref, up, down):
    width = up.shape[1]
    before_act = lax.dot_general(rows_ref[:, :width], up, NT, preferred_element_type=f32)
    lifted = lax.dot_general(rows_ref[:, width:2 * width], up, NT, preferred_element_type=f32)
    pulled = lax.dot_general(rows_ref[:, 2 * width:], down, NT, preferred_element_type=f32)
    return (pulled * curvature(before_act) * lifted).astype(bf16)


def accumulate(rows_ref, ups, downs, total=None):
    inners = [inner_of(rows_ref, up[...], down[...]) for up, down in zip(ups, downs)]
    for inner, up in zip(inners, ups):
        part = jnp.dot(inner, up[...], preferred_element_type=f32)
        total = part if total is None else total + part
    return total


def own_kernel(n_w, own_ref, *refs):
    ups, downs = refs[:n_w], refs[n_w:2 * n_w]
    acc_ref, own_out, up_out, down_out, sems = refs[-5:]
    own_copy = pltpu.make_async_copy(own_ref, own_out, sems.at[0])
    copies = []
    for g in range(n_w):
        copies.append(pltpu.make_async_copy(ups[g], up_out.at[g], sems.at[1 + 2 * g]))
        copies.append(pltpu.make_async_copy(downs[g], down_out.at[g], sems.at[2 + 2 * g]))
    for copy in (own_copy, *copies[:4]):
        copy.start()
    for copy in (own_copy, *copies[:2]):
        copy.wait()
    for copy in copies[4:]:
        copy.start()
    total = accumulate(own_out, [up_out.at[0]], [down_out.at[0]])
    for copy in copies[2:]:
        copy.wait()
    rest = range(1, n_w)
    acc_ref[...] = accumulate(own_out, [up_out.at[g] for g in rest], [down_out.at[g] for g in rest], total)


def own_call(own, ups, downs, mark):
    rows, width = own.shape[0], own.shape[1] // 3
    n_w = len(ups)
    stack = jax.ShapeDtypeStruct((n_w, *ups[0].shape), bf16)
    operands = (own, *ups, *downs, mark)
    return pl.pallas_call(
        functools.partial(own_kernel, n_w),
        out_shape=(jax.ShapeDtypeStruct((rows, width), f32), jax.ShapeDtypeStruct(own.shape, bf16), stack, stack),
        in_specs=[ANY] * len(operands),
        out_specs=(VMEM,) * 4,
        scratch_shapes=[pltpu.SemaphoreType.DMA((2 * n_w + 1,))],
        compiler_params=params(16),
    )(*operands)


def other_kernel(other_ref, up_ref, down_ref, acc_ref, other_out, sem):
    copy = pltpu.make_async_copy(other_ref, other_out, sem)
    copy.start()
    copy.wait()
    blocks = range(up_ref.shape[0])
    acc_ref[...] = accumulate(other_out, [up_ref.at[g] for g in blocks], [down_ref.at[g] for g in blocks])


def other_call(other, up_stack, down_stack):
    rows, width = other.shape[0], other.shape[1] // 3
    stacks = [pltpu.with_memory_space_constraint(x, pltpu.VMEM) for x in (up_stack, down_stack)]
    return pl.pallas_call(
        other_kernel,
        out_shape=(jax.ShapeDtypeStruct((rows, width), f32), jax.ShapeDtypeStruct(other.shape, bf16)),
        in_specs=[ANY, VMEM, VMEM],
        out_specs=(VMEM, VMEM),
        scratch_shapes=[pltpu.SemaphoreType.DMA],
        compiler_params=params(16),
    )(other, *stacks)


def next_kernel(n_w, own_ref, other_ref, *refs):
    ups, downs, accs = refs[:n_w], refs[n_w:2 * n_w], refs[2 * n_w:2 * n_w + 2]
    outs, up_buf, down_buf, sems = refs[-5:-3], *refs[-3:]
    copies = []
    for g in range(n_w):
        copies.append(pltpu.make_async_copy(ups[g], up_buf.at[g], sems.at[2 * g]))
        copies.append(pltpu.make_async_copy(downs[g], down_buf.at[g], sems.at[2 * g + 1]))
    for copy in copies:
        copy.start()
    for copy in copies:
        copy.wait()
    blocks = range(n_w)
    for rows_ref, acc_ref, out_ref in zip((own_ref, other_ref), accs, outs):
        total = accumulate(rows_ref, [up_buf.at[g] for g in blocks], [down_buf.at[g] for g in blocks], acc_ref[...])
        out_ref[...] = total.astype(out_ref.dtype)


def next_call(rows, ups, downs, acc, mark):
    n_w = len(ups)
    inside = [pltpu.with_memory_space_constraint(x, pltpu.VMEM) for x in (*rows, *acc)]
    return pl.pallas_call(
        functools.partial(next_kernel, n_w),
        out_shape=tuple(jax.ShapeDtypeStruct(x.shape, kind) for x, kind in zip(acc, (f32, bf16))),
        in_specs=[VMEM] * 2 + [ANY] * (2 * n_w) + [VMEM] * 2 + [ANY],
        out_specs=(VMEM,) * 2,
        scratch_shapes=[
            pltpu.VMEM((n_w, *ups[0].shape), bf16),
            pltpu.VMEM((n_w, *ups[0].shape), bf16),
            pltpu.SemaphoreType.DMA((2 * n_w,)),
        ],
        compiler_params=params(20),
    )(*inside[:2], *ups, *downs, *inside[2:], mark)


def factor_kernel(rows_ref, up_ref, factor_ref):
    width = up_ref.shape[1]
    before_act = lax.dot_general(rows_ref[:, :width], up_ref[...], NT, preferred_element_type=f32)
    lifted = lax.dot_general(rows_ref[:, width:2 * width], up_ref[...], NT, preferred_element_type=f32)
    factor_ref[...] = curvature(before_act) * lifted


def last_kernel(rows_ref, factor_ref, up_ref, down_ref, *refs):
    totals, out_ref = refs[:-1], refs[-1]
    width = up_ref.shape[1]
    pulled = lax.dot_general(rows_ref[:, 2 * width:], down_ref[...], NT, preferred_element_type=f32)
    inner = (pulled * factor_ref[...]).astype(bf16)
    total = jnp.dot(inner, up_ref[...], preferred_element_type=f32)
    for ref in totals:
        total = total + ref[...].astype(f32)
    out_ref[...] = total.astype(out_ref.dtype)


def last_call(kernel, shape, kind, *operands):
    operands = tuple(pltpu.with_memory_space_constraint(x, pltpu.VMEM) for x in operands)
    return pl.pallas_call(
        kernel,
        out_shape=jax.ShapeDtypeStruct(shape, kind),
        in_specs=[VMEM] * len(operands),
        out_specs=VMEM,
        compiler_params=params(12),
    )(*operands)


def hold_kernel(*refs):
    refs[-1][...] = jnp.zeros_like(refs[-1])


def hold(*arrays):
    return pl.pallas_call(
        hold_kernel,
        out_shape=jax.ShapeDtypeStruct((8, 128), f32),
        in_specs=[ANY] * len(arrays),
        out_specs=VMEM,
        compiler_params=params(1),
        cost_estimate=pl.CostEstimate(flops=200_000_000_000, bytes_accessed=1_000_000_000, transcendentals=0),
    )(*arrays)


def local(tokens, tangent, cotangent, routes, gate_num, w_up, w_down):
    n_dp = lax.axis_size("dp")
    experts = lax.axis_size("expert")
    width = tokens.shape[1]
    forth = [(i, (i + 2) % n_dp) for i in range(n_dp)]
    back = [(i, (i - 2) % n_dp) for i in range(n_dp)]
    swap = [(i, i ^ 1) for i in range(n_dp)]
    up0, down0 = w_up[0], w_down[0]

    def send_on(x, way):
        return lax.ppermute(x, "dp", way)

    after = lax.optimization_barrier
    uf1, db1 = send_on(up0, forth), send_on(down0, back)
    df1, ub1 = send_on(down0, forth), send_on(up0, back)
    send, mix = prepare(routes, gate_num, tokens, tangent, cotangent, experts)
    own = lax.all_to_all(send.reshape(experts, CAP, 3 * width), "expert", 0, 0, tiled=True)
    own = own.reshape(experts * CAP, 3 * width)
    mark = hold(uf1)
    uf1, db1, mark = after((uf1, db1, mark))
    uf2, db2 = send_on(uf1, forth), send_on(db1, back)
    df1, ub1, mark = after((df1, ub1, mark))
    df2, ub2 = send_on(df1, forth), send_on(ub1, back)
    uf2, db2, df1, ub1 = after((uf2, db2, df1, ub1))
    uf3, db3 = send_on(uf2, forth), send_on(db2, back)
    df2, ub2, uf2, db2 = after((df2, ub2, uf2, db2))
    df3, ub3 = send_on(df2, forth), send_on(ub2, back)
    mine, kept_own, up_stack, down_stack = own_call(own, (up0, uf1, ub1, uf2, ub2), (down0, df1, db1, df2, db2), mark)
    mark3 = hold(uf3, kept_own)
    uf3, db3, df2, ub2, mark3 = after((uf3, db3, df2, ub2, mark3))
    uf4, db4 = send_on(uf3, forth), send_on(db3, back)
    other = lax.ppermute(own, "dp", swap)
    theirs, kept_other = other_call(other, up_stack, down_stack)
    mine, theirs = next_call((kept_own, kept_other), (uf3, ub3), (df3, db3), (mine, theirs), mark3)
    passed = send_on(theirs, swap)
    far_up = send_on(uf4, swap)
    uf4, mine = after((uf4, mine))
    shape = (own.shape[0], uf4.shape[0])
    factor = last_call(factor_kernel, shape, f32, kept_own, uf4)
    db4, factor = after((db4, factor))
    far_down = send_on(db4, swap)
    part = last_call(last_kernel, mine.shape, f32, kept_own, factor, uf4, db4, mine)
    far_up, part = after((far_up, part))
    factor = last_call(factor_kernel, shape, f32, kept_own, far_up)
    whole = last_call(last_kernel, mine.shape, bf16, kept_own, factor, far_up, far_down, part, passed)
    returned = lax.all_to_all(whole.reshape(experts, CAP, width), "expert", 0, 0, tiled=True)
    returned = returned.reshape(experts * CAP, width)
    return lax.dot_general(mix, returned, (((0,), (0,)), ((), ())), preferred_element_type=f32)


def solution(mesh):
    tok = P(("dp", "expert"), None)
    w = P("expert", "dp", None)
    return jax.shard_map(
        local, mesh=mesh, in_specs=(tok,) * 5 + (w, w), out_specs=tok, check_vma=False
    )
```

```python
import functools

import jax
import jax.numpy as jnp
from jax import lax
from jax.experimental import pallas as pl
from jax.experimental.pallas import tpu as pltpu
from jax.sharding import PartitionSpec as P

f32, bf16 = jnp.float32, jnp.bfloat16
CAP = 24
NT = (((1,), (1,)), ((), ()))
VMEM = pl.BlockSpec(memory_space=pltpu.VMEM)
ANY = pl.BlockSpec(memory_space=pl.ANY)


def params(mib):
    return pltpu.CompilerParams(vmem_limit_bytes=mib << 20)


def curvature(x):
    t = jnp.tanh(0.5 * x)
    return (0.25 - 0.25 * t * t) * (2.0 - x * t)


def prepare_kernel(routes_hbm, gates_hbm, x_hbm, t_hbm, c_hbm, send_hbm, mix_ref, routes, gates, rows, send, sems):
    slots, n = mix_ref.shape
    small = [pltpu.make_async_copy(routes_hbm, routes, sems.at[0]), pltpu.make_async_copy(gates_hbm, gates, sems.at[1])]
    big = [pltpu.make_async_copy(ref, rows.at[i], sems.at[2 + i]) for i, ref in enumerate((x_hbm, t_hbm, c_hbm))]
    width = rows.shape[2]
    leave = [
        pltpu.make_async_copy(send.at[i], send_hbm.at[:, i * width:(i + 1) * width], sems.at[5 + i]) for i in range(3)
    ]
    for copy in small + big:
        copy.start()
    for copy in small:
        copy.wait()
    slot = lax.broadcasted_iota(jnp.int32, (slots, n), 0)
    expert = (slot * 2731) >> 16
    place = slot - expert * CAP
    first, second = routes[0:1, :] == expert, routes[1:2, :] == expert
    named = (first | second).astype(f32)
    earlier = lax.broadcasted_iota(jnp.int32, (n, n), 0) < lax.broadcasted_iota(jnp.int32, (n, n), 1)
    before = jnp.dot(named.astype(bf16), earlier.astype(f32).astype(bf16), preferred_element_type=f32)
    here = before.astype(jnp.int32) == place
    pick = jnp.where(here, named, 0.0).astype(bf16)
    for i in range(3):
        big[i].wait()
        send[i] = jnp.dot(pick, rows[i], preferred_element_type=f32).astype(bf16)
        leave[i].start()
    weights = gates[...].astype(f32) / 64.0
    weight = jnp.where(first, weights[0:1, :], 0.0) + jnp.where(second, weights[1:2, :], 0.0)
    mix_ref[...] = jnp.where(here, weight, 0.0).astype(bf16)
    for copy in leave:
        copy.wait()


def prepare(routes, gate_num, tokens, tangent, cotangent, experts):
    n, width = tokens.shape
    slots = experts * CAP
    return pl.pallas_call(
        prepare_kernel,
        out_shape=(
            jax.ShapeDtypeStruct((slots, 3 * width), bf16),
            jax.ShapeDtypeStruct((slots, n), bf16),
        ),
        in_specs=[ANY] * 5,
        out_specs=(ANY, VMEM),
        scratch_shapes=[
            pltpu.VMEM((2, n), jnp.int32),
            pltpu.VMEM((2, n), jnp.int32),
            pltpu.VMEM((3, n, width), bf16),
            pltpu.VMEM((3, slots, width), bf16),
            pltpu.SemaphoreType.DMA((8,)),
        ],
        compiler_params=params(16),
    )(*(pltpu.with_memory_space_constraint(a, pltpu.HBM) for a in (routes.T, gate_num.T, tokens, tangent, cotangent)))


def inner_of(rows_ref, up, down):
    width = up.shape[1]
    before_act = lax.dot_general(rows_ref[:, :width], up, NT, preferred_element_type=f32)
    lifted = lax.dot_general(rows_ref[:, width:2 * width], up, NT, preferred_element_type=f32)
    pulled = lax.dot_general(rows_ref[:, 2 * width:], down, NT, preferred_element_type=f32)
    return (pulled * curvature(before_act) * lifted).astype(bf16)


def accumulate(rows_ref, ups, downs, total=None):
    inners = [inner_of(rows_ref, up[...], down[...]) for up, down in zip(ups, downs)]
    for inner, up in zip(inners, ups):
        part = jnp.dot(inner, up[...], preferred_element_type=f32)
        total = part if total is None else total + part
    return total


def own_kernel(n_w, own_ref, *refs):
    ups, downs = refs[:n_w], refs[n_w:2 * n_w]
    acc_ref, own_out, up_out, down_out, sems = refs[-5:]
    own_copy = pltpu.make_async_copy(own_ref, own_out, sems.at[0])
    copies = []
    for g in range(n_w):
        copies.append(pltpu.make_async_copy(ups[g], up_out.at[g], sems.at[1 + 2 * g]))
        copies.append(pltpu.make_async_copy(downs[g], down_out.at[g], sems.at[2 + 2 * g]))
    for copy in (own_copy, *copies[:4]):
        copy.start()
    for copy in (own_copy, *copies[:2]):
        copy.wait()
    for copy in copies[4:]:
        copy.start()
    total = accumulate(own_out, [up_out.at[0]], [down_out.at[0]])
    for copy in copies[2:]:
        copy.wait()
    rest = range(1, n_w)
    acc_ref[...] = accumulate(own_out, [up_out.at[g] for g in rest], [down_out.at[g] for g in rest], total)


def own_call(own, ups, downs, mark):
    rows, width = own.shape[0], own.shape[1] // 3
    n_w = len(ups)
    stack = jax.ShapeDtypeStruct((n_w, *ups[0].shape), bf16)
    operands = (own, *ups, *downs, mark)
    return pl.pallas_call(
        functools.partial(own_kernel, n_w),
        out_shape=(jax.ShapeDtypeStruct((rows, width), f32), jax.ShapeDtypeStruct(own.shape, bf16), stack, stack),
        in_specs=[ANY] * len(operands),
        out_specs=(VMEM,) * 4,
        scratch_shapes=[pltpu.SemaphoreType.DMA((2 * n_w + 1,))],
        compiler_params=params(16),
    )(*operands)


def other_kernel(other_ref, up_ref, down_ref, acc_ref, other_out, sem):
    copy = pltpu.make_async_copy(other_ref, other_out, sem)
    copy.start()
    copy.wait()
    blocks = range(up_ref.shape[0])
    acc_ref[...] = accumulate(other_out, [up_ref.at[g] for g in blocks], [down_ref.at[g] for g in blocks])


def other_call(other, up_stack, down_stack):
    rows, width = other.shape[0], other.shape[1] // 3
    stacks = [pltpu.with_memory_space_constraint(x, pltpu.VMEM) for x in (up_stack, down_stack)]
    return pl.pallas_call(
        other_kernel,
        out_shape=(jax.ShapeDtypeStruct((rows, width), f32), jax.ShapeDtypeStruct(other.shape, bf16)),
        in_specs=[ANY, VMEM, VMEM],
        out_specs=(VMEM, VMEM),
        scratch_shapes=[pltpu.SemaphoreType.DMA],
        compiler_params=params(16),
    )(other, *stacks)


def next_kernel(n_w, own_ref, other_ref, *refs):
    ups, downs, accs = refs[:n_w], refs[n_w:2 * n_w], refs[2 * n_w:2 * n_w + 2]
    outs, up_buf, down_buf, sems = refs[-5:-3], *refs[-3:]
    copies = []
    for g in range(n_w):
        copies.append(pltpu.make_async_copy(ups[g], up_buf.at[g], sems.at[2 * g]))
        copies.append(pltpu.make_async_copy(downs[g], down_buf.at[g], sems.at[2 * g + 1]))
    for copy in copies:
        copy.start()
    for copy in copies:
        copy.wait()
    blocks = range(n_w)
    for rows_ref, acc_ref, out_ref in zip((own_ref, other_ref), accs, outs):
        total = accumulate(rows_ref, [up_buf.at[g] for g in blocks], [down_buf.at[g] for g in blocks], acc_ref[...])
        out_ref[...] = total.astype(out_ref.dtype)


def next_call(rows, ups, downs, acc, mark):
    n_w = len(ups)
    inside = [pltpu.with_memory_space_constraint(x, pltpu.VMEM) for x in (*rows, *acc)]
    return pl.pallas_call(
        functools.partial(next_kernel, n_w),
        out_shape=tuple(jax.ShapeDtypeStruct(x.shape, kind) for x, kind in zip(acc, (f32, bf16))),
        in_specs=[VMEM] * 2 + [ANY] * (2 * n_w) + [VMEM] * 2 + [ANY],
        out_specs=(VMEM,) * 2,
        scratch_shapes=[
            pltpu.VMEM((n_w, *ups[0].shape), bf16),
            pltpu.VMEM((n_w, *ups[0].shape), bf16),
            pltpu.SemaphoreType.DMA((2 * n_w,)),
        ],
        compiler_params=params(20),
    )(*inside[:2], *ups, *downs, *inside[2:], mark)


def last_own_kernel(rows_ref, up_ref, down_ref, acc_ref, out_ref):
    out_ref[...] = accumulate(rows_ref, [up_ref], [down_ref], acc_ref[...])


def last_far_kernel(rows_ref, up_ref, down_ref, acc_ref, passed_ref, out_ref):
    total = acc_ref[...] + passed_ref[...].astype(f32)
    out_ref[...] = accumulate(rows_ref, [up_ref], [down_ref], total).astype(out_ref.dtype)


def last_call(kernel, shape, kind, *operands):
    operands = tuple(pltpu.with_memory_space_constraint(x, pltpu.VMEM) for x in operands)
    return pl.pallas_call(
        kernel,
        out_shape=jax.ShapeDtypeStruct(shape, kind),
        in_specs=[VMEM] * len(operands),
        out_specs=VMEM,
        compiler_params=params(12),
    )(*operands)


def hold_kernel(*refs):
    refs[-1][...] = jnp.zeros_like(refs[-1])


def hold(*arrays):
    return pl.pallas_call(
        hold_kernel,
        out_shape=jax.ShapeDtypeStruct((8, 128), f32),
        in_specs=[ANY] * len(arrays),
        out_specs=VMEM,
        compiler_params=params(1),
        cost_estimate=pl.CostEstimate(flops=200_000_000_000, bytes_accessed=1_000_000_000, transcendentals=0),
    )(*arrays)


def local(tokens, tangent, cotangent, routes, gate_num, w_up, w_down):
    n_dp = lax.axis_size("dp")
    experts = lax.axis_size("expert")
    width = tokens.shape[1]
    forth = [(i, (i + 2) % n_dp) for i in range(n_dp)]
    back = [(i, (i - 2) % n_dp) for i in range(n_dp)]
    swap = [(i, i ^ 1) for i in range(n_dp)]
    up0, down0 = w_up[0], w_down[0]

    def send_on(x, way):
        return lax.ppermute(x, "dp", way)

    after = lax.optimization_barrier
    uf1, db1 = send_on(up0, forth), send_on(down0, back)
    df1, ub1 = send_on(down0, forth), send_on(up0, back)
    send, mix = prepare(routes, gate_num, tokens, tangent, cotangent, experts)
    own = lax.all_to_all(send.reshape(experts, CAP, 3 * width), "expert", 0, 0, tiled=True)
    own = own.reshape(experts * CAP, 3 * width)
    mark = hold(uf1)
    uf1, db1, mark = after((uf1, db1, mark))
    uf2, db2 = send_on(uf1, forth), send_on(db1, back)
    df1, ub1, mark = after((df1, ub1, mark))
    df2, ub2 = send_on(df1, forth), send_on(ub1, back)
    uf2, db2, df1, ub1 = after((uf2, db2, df1, ub1))
    uf3, db3 = send_on(uf2, forth), send_on(db2, back)
    df2, ub2, uf2, db2 = after((df2, ub2, uf2, db2))
    df3, ub3 = send_on(df2, forth), send_on(ub2, back)
    mine, kept_own, up_stack, down_stack = own_call(own, (up0, uf1, ub1, uf2, ub2), (down0, df1, db1, df2, db2), mark)
    mark3 = hold(uf3, kept_own)
    uf3, db3, df2, ub2, mark3 = after((uf3, db3, df2, ub2, mark3))
    uf4, db4 = send_on(uf3, forth), send_on(db3, back)
    other = lax.ppermute(own, "dp", swap)
    theirs, kept_other = other_call(other, up_stack, down_stack)
    mine, theirs = next_call((kept_own, kept_other), (uf3, ub3), (df3, db3), (mine, theirs), mark3)
    passed = send_on(theirs, swap)
    far_up, far_down = send_on(uf4, swap), send_on(db4, swap)
    part = last_call(last_own_kernel, mine.shape, f32, kept_own, uf4, db4, mine)
    far_up, far_down, part = after((far_up, far_down, part))
    whole = last_call(last_far_kernel, mine.shape, bf16, kept_own, far_up, far_down, part, passed)
    returned = lax.all_to_all(whole.reshape(experts, CAP, width), "expert", 0, 0, tiled=True)
    returned = returned.reshape(experts * CAP, width)
    return lax.dot_general(mix, returned, (((0,), (0,)), ((), ())), preferred_element_type=f32)


def solution(mesh):
    tok = P(("dp", "expert"), None)
    w = P("expert", "dp", None)
    return jax.shard_map(
        local, mesh=mesh, in_specs=(tok,) * 5 + (w, w), out_specs=tok, check_vma=False
    )
```

```python
import functools

import jax
import jax.numpy as jnp
from jax import lax
from jax.experimental import pallas as pl
from jax.experimental.pallas import tpu as pltpu
from jax.sharding import PartitionSpec as P

f32, bf16 = jnp.float32, jnp.bfloat16
CAP = 24
NT = (((1,), (1,)), ((), ()))
VMEM = pl.BlockSpec(memory_space=pltpu.VMEM)
ANY = pl.BlockSpec(memory_space=pl.ANY)


def params(mib):
    return pltpu.CompilerParams(vmem_limit_bytes=mib << 20)


def curvature(x):
    t = jnp.tanh(0.5 * x)
    return (0.25 - 0.25 * t * t) * (2.0 - x * t)


def prepare_kernel(routes_hbm, gates_hbm, x_hbm, t_hbm, c_hbm, send_hbm, mix_ref, routes, gates, rows, send, sems):
    slots, n = mix_ref.shape
    small = [pltpu.make_async_copy(routes_hbm, routes, sems.at[0]), pltpu.make_async_copy(gates_hbm, gates, sems.at[1])]
    big = [pltpu.make_async_copy(ref, rows.at[i], sems.at[2 + i]) for i, ref in enumerate((x_hbm, t_hbm, c_hbm))]
    width = rows.shape[2]
    leave = [
        pltpu.make_async_copy(send.at[i], send_hbm.at[:, i * width:(i + 1) * width], sems.at[5 + i]) for i in range(3)
    ]
    for copy in small + big:
        copy.start()
    for copy in small:
        copy.wait()
    slot = lax.broadcasted_iota(jnp.int32, (slots, n), 0)
    expert = (slot * 2731) >> 16
    place = slot - expert * CAP
    first, second = routes[0:1, :] == expert, routes[1:2, :] == expert
    named = (first | second).astype(f32)
    earlier = lax.broadcasted_iota(jnp.int32, (n, n), 0) < lax.broadcasted_iota(jnp.int32, (n, n), 1)
    before = jnp.dot(named.astype(bf16), earlier.astype(f32).astype(bf16), preferred_element_type=f32)
    here = before.astype(jnp.int32) == place
    pick = jnp.where(here, named, 0.0).astype(bf16)
    for i in range(3):
        big[i].wait()
        send[i] = jnp.dot(pick, rows[i], preferred_element_type=f32).astype(bf16)
        leave[i].start()
    weights = gates[...].astype(f32) / 64.0
    weight = jnp.where(first, weights[0:1, :], 0.0) + jnp.where(second, weights[1:2, :], 0.0)
    mix_ref[...] = jnp.where(here, weight, 0.0).astype(bf16)
    for copy in leave:
        copy.wait()


def prepare(routes, gate_num, tokens, tangent, cotangent, experts):
    n, width = tokens.shape
    slots = experts * CAP
    return pl.pallas_call(
        prepare_kernel,
        out_shape=(
            jax.ShapeDtypeStruct((slots, 3 * width), bf16),
            jax.ShapeDtypeStruct((slots, n), bf16),
        ),
        in_specs=[ANY] * 5,
        out_specs=(ANY, VMEM),
        scratch_shapes=[
            pltpu.VMEM((2, n), jnp.int32),
            pltpu.VMEM((2, n), jnp.int32),
            pltpu.VMEM((3, n, width), bf16),
            pltpu.VMEM((3, slots, width), bf16),
            pltpu.SemaphoreType.DMA((8,)),
        ],
        compiler_params=params(16),
    )(*(pltpu.with_memory_space_constraint(a, pltpu.HBM) for a in (routes.T, gate_num.T, tokens, tangent, cotangent)))


def inner_of(rows_ref, up, down):
    width = up.shape[1]
    before_act = lax.dot_general(rows_ref[:, :width], up, NT, preferred_element_type=f32)
    lifted = lax.dot_general(rows_ref[:, width:2 * width], up, NT, preferred_element_type=f32)
    pulled = lax.dot_general(rows_ref[:, 2 * width:], down, NT, preferred_element_type=f32)
    return (pulled * curvature(before_act) * lifted).astype(bf16)


def accumulate(rows_ref, ups, downs, total=None):
    inners = [inner_of(rows_ref, up[...], down[...]) for up, down in zip(ups, downs)]
    for inner, up in zip(inners, ups):
        part = jnp.dot(inner, up[...], preferred_element_type=f32)
        total = part if total is None else total + part
    return total


def own_kernel(n_w, own_ref, *refs):
    ups, downs = refs[:n_w], refs[n_w:2 * n_w]
    acc_ref, own_out, up_out, down_out, sems = refs[-5:]
    own_copy = pltpu.make_async_copy(own_ref, own_out, sems.at[0])
    copies = []
    for g in range(n_w):
        copies.append(pltpu.make_async_copy(ups[g], up_out.at[g], sems.at[1 + 2 * g]))
        copies.append(pltpu.make_async_copy(downs[g], down_out.at[g], sems.at[2 + 2 * g]))
    for copy in (own_copy, *copies[:4]):
        copy.start()
    for copy in (own_copy, *copies[:2]):
        copy.wait()
    for copy in copies[4:]:
        copy.start()
    total = accumulate(own_out, [up_out.at[0]], [down_out.at[0]])
    for copy in copies[2:]:
        copy.wait()
    rest = range(1, n_w)
    acc_ref[...] = accumulate(own_out, [up_out.at[g] for g in rest], [down_out.at[g] for g in rest], total)


def own_call(own, ups, downs, mark):
    rows, width = own.shape[0], own.shape[1] // 3
    n_w = len(ups)
    stack = jax.ShapeDtypeStruct((n_w, *ups[0].shape), bf16)
    operands = (own, *ups, *downs, mark)
    return pl.pallas_call(
        functools.partial(own_kernel, n_w),
        out_shape=(jax.ShapeDtypeStruct((rows, width), f32), jax.ShapeDtypeStruct(own.shape, bf16), stack, stack),
        in_specs=[ANY] * len(operands),
        out_specs=(VMEM,) * 4,
        scratch_shapes=[pltpu.SemaphoreType.DMA((2 * n_w + 1,))],
        compiler_params=params(16),
    )(*operands)


def other_kernel(other_ref, up_ref, down_ref, acc_ref, other_out, sem):
    copy = pltpu.make_async_copy(other_ref, other_out, sem)
    copy.start()
    copy.wait()
    blocks = range(up_ref.shape[0])
    acc_ref[...] = accumulate(other_out, [up_ref.at[g] for g in blocks], [down_ref.at[g] for g in blocks])


def other_call(other, up_stack, down_stack):
    rows, width = other.shape[0], other.shape[1] // 3
    stacks = [pltpu.with_memory_space_constraint(x, pltpu.VMEM) for x in (up_stack, down_stack)]
    return pl.pallas_call(
        other_kernel,
        out_shape=(jax.ShapeDtypeStruct((rows, width), f32), jax.ShapeDtypeStruct(other.shape, bf16)),
        in_specs=[ANY, VMEM, VMEM],
        out_specs=(VMEM, VMEM),
        scratch_shapes=[pltpu.SemaphoreType.DMA],
        compiler_params=params(16),
    )(other, *stacks)


def next_kernel(n_w, own_ref, other_ref, *refs):
    ups, downs, accs = refs[:n_w], refs[n_w:2 * n_w], refs[2 * n_w:2 * n_w + 2]
    outs, up_buf, down_buf, sems = refs[-5:-3], *refs[-3:]
    copies = []
    for g in range(n_w):
        copies.append(pltpu.make_async_copy(ups[g], up_buf.at[g], sems.at[2 * g]))
        copies.append(pltpu.make_async_copy(downs[g], down_buf.at[g], sems.at[2 * g + 1]))
    for copy in copies:
        copy.start()
    for copy in copies:
        copy.wait()
    blocks = range(n_w)
    for rows_ref, acc_ref, out_ref in zip((own_ref, other_ref), accs, outs):
        total = accumulate(rows_ref, [up_buf.at[g] for g in blocks], [down_buf.at[g] for g in blocks], acc_ref[...])
        out_ref[...] = total.astype(out_ref.dtype)


def next_call(rows, ups, downs, acc, mark):
    n_w = len(ups)
    inside = [pltpu.with_memory_space_constraint(x, pltpu.VMEM) for x in (*rows, *acc)]
    return pl.pallas_call(
        functools.partial(next_kernel, n_w),
        out_shape=tuple(jax.ShapeDtypeStruct(x.shape, kind) for x, kind in zip(acc, (f32, bf16))),
        in_specs=[VMEM] * 2 + [ANY] * (2 * n_w) + [VMEM] * 2 + [ANY],
        out_specs=(VMEM,) * 2,
        scratch_shapes=[
            pltpu.VMEM((n_w, *ups[0].shape), bf16),
            pltpu.VMEM((n_w, *ups[0].shape), bf16),
            pltpu.SemaphoreType.DMA((2 * n_w,)),
        ],
        compiler_params=params(20),
    )(*inside[:2], *ups, *downs, *inside[2:], mark)


def factor_kernel(rows_ref, up_ref, factor_ref):
    width = up_ref.shape[1]
    before_act = lax.dot_general(rows_ref[:, :width], up_ref[...], NT, preferred_element_type=f32)
    lifted = lax.dot_general(rows_ref[:, width:2 * width], up_ref[...], NT, preferred_element_type=f32)
    factor_ref[...] = curvature(before_act) * lifted


def last_own_kernel(rows_ref, up_ref, down_ref, acc_ref, out_ref):
    out_ref[...] = accumulate(rows_ref, [up_ref], [down_ref], acc_ref[...])


def last_far_kernel(rows_ref, factor_ref, up_ref, down_ref, acc_ref, passed_ref, out_ref):
    width = up_ref.shape[1]
    pulled = lax.dot_general(rows_ref[:, 2 * width:], down_ref[...], NT, preferred_element_type=f32)
    inner = (pulled * factor_ref[...]).astype(bf16)
    total = acc_ref[...] + passed_ref[...].astype(f32)
    out_ref[...] = (total + jnp.dot(inner, up_ref[...], preferred_element_type=f32)).astype(out_ref.dtype)


def last_call(kernel, shape, kind, *operands):
    operands = tuple(pltpu.with_memory_space_constraint(x, pltpu.VMEM) for x in operands)
    return pl.pallas_call(
        kernel,
        out_shape=jax.ShapeDtypeStruct(shape, kind),
        in_specs=[VMEM] * len(operands),
        out_specs=VMEM,
        compiler_params=params(12),
    )(*operands)


def mix_kernel(mix_ref, returned_ref, out_ref):
    contract = (((0,), (0,)), ((), ()))
    out_ref[...] = lax.dot_general(mix_ref[...], returned_ref[...], contract, preferred_element_type=f32)


def mix_call(mix, returned):
    slots, n = mix.shape
    width = returned.shape[1]
    return pl.pallas_call(
        mix_kernel,
        out_shape=jax.ShapeDtypeStruct((n, width), f32),
        in_specs=[VMEM, VMEM],
        out_specs=VMEM,
        compiler_params=params(8),
    )(*(pltpu.with_memory_space_constraint(x, pltpu.VMEM) for x in (mix, returned)))


def hold_kernel(*refs):
    refs[-1][...] = jnp.zeros_like(refs[-1])


def hold(*arrays):
    return pl.pallas_call(
        hold_kernel,
        out_shape=jax.ShapeDtypeStruct((8, 128), f32),
        in_specs=[ANY] * len(arrays),
        out_specs=VMEM,
        compiler_params=params(1),
        cost_estimate=pl.CostEstimate(flops=200_000_000_000, bytes_accessed=1_000_000_000, transcendentals=0),
    )(*arrays)


def local(tokens, tangent, cotangent, routes, gate_num, w_up, w_down):
    n_dp = lax.axis_size("dp")
    experts = lax.axis_size("expert")
    width = tokens.shape[1]
    forth = [(i, (i + 2) % n_dp) for i in range(n_dp)]
    back = [(i, (i - 2) % n_dp) for i in range(n_dp)]
    swap = [(i, i ^ 1) for i in range(n_dp)]
    up0, down0 = w_up[0], w_down[0]

    def send_on(x, way):
        return lax.ppermute(x, "dp", way)

    after = lax.optimization_barrier
    uf1, db1 = send_on(up0, forth), send_on(down0, back)
    df1, ub1 = send_on(down0, forth), send_on(up0, back)
    send, mix = prepare(routes, gate_num, tokens, tangent, cotangent, experts)
    own = lax.all_to_all(send.reshape(experts, CAP, 3 * width), "expert", 0, 0, tiled=True)
    own = own.reshape(experts * CAP, 3 * width)
    mark = hold(uf1)
    uf1, db1, mark = after((uf1, db1, mark))
    uf2, db2 = send_on(uf1, forth), send_on(db1, back)
    df1, ub1, mark = after((df1, ub1, mark))
    df2, ub2 = send_on(df1, forth), send_on(ub1, back)
    uf2, db2, df1, ub1 = after((uf2, db2, df1, ub1))
    uf3, db3 = send_on(uf2, forth), send_on(db2, back)
    df2, ub2, uf2, db2 = after((df2, ub2, uf2, db2))
    df3, ub3 = send_on(df2, forth), send_on(ub2, back)
    mine, kept_own, up_stack, down_stack = own_call(own, (up0, uf1, ub1, uf2, ub2), (down0, df1, db1, df2, db2), mark)
    mark3 = hold(uf3, kept_own)
    uf3, db3, df2, ub2, mark3 = after((uf3, db3, df2, ub2, mark3))
    uf4, db4 = send_on(uf3, forth), send_on(db3, back)
    other = lax.ppermute(own, "dp", swap)
    theirs, kept_other = other_call(other, up_stack, down_stack)
    mine, theirs = next_call((kept_own, kept_other), (uf3, ub3), (df3, db3), (mine, theirs), mark3)
    passed = send_on(theirs, swap)
    far_up, far_down = send_on(uf4, swap), send_on(db4, swap)
    part = last_call(last_own_kernel, mine.shape, f32, kept_own, uf4, db4, mine)
    far_up, part = after((far_up, part))
    factor = last_call(factor_kernel, (own.shape[0], far_up.shape[0]), f32, kept_own, far_up)
    whole = last_call(last_far_kernel, mine.shape, bf16, kept_own, factor, far_up, far_down, part, passed)
    returned = lax.all_to_all(whole.reshape(experts, CAP, width), "expert", 0, 0, tiled=True)
    returned = returned.reshape(experts * CAP, width)
    return mix_call(mix, returned)


def solution(mesh):
    tok = P(("dp", "expert"), None)
    w = P("expert", "dp", None)
    return jax.shard_map(
        local, mesh=mesh, in_specs=(tok,) * 5 + (w, w), out_specs=tok, check_vma=False
    )
```

```python
import functools

import jax
import jax.numpy as jnp
from jax import lax
from jax.experimental import pallas as pl
from jax.experimental.pallas import tpu as pltpu
from jax.sharding import PartitionSpec as P

f32, bf16 = jnp.float32, jnp.bfloat16
CAP = 24
NT = (((1,), (1,)), ((), ()))
VMEM = pl.BlockSpec(memory_space=pltpu.VMEM)
ANY = pl.BlockSpec(memory_space=pl.ANY)


def params(mib):
    return pltpu.CompilerParams(vmem_limit_bytes=mib << 20)


def curvature(x):
    t = jnp.tanh(0.5 * x)
    return (0.25 - 0.25 * t * t) * (2.0 - x * t)


def prepare_kernel(routes_hbm, gates_hbm, x_hbm, t_hbm, c_hbm, send_hbm, mix_ref, routes, gates, rows, send, sems):
    slots, n = mix_ref.shape
    small = [pltpu.make_async_copy(routes_hbm, routes, sems.at[0]), pltpu.make_async_copy(gates_hbm, gates, sems.at[1])]
    big = [pltpu.make_async_copy(ref, rows.at[i], sems.at[2 + i]) for i, ref in enumerate((x_hbm, t_hbm, c_hbm))]
    width = rows.shape[2]
    leave = [
        pltpu.make_async_copy(send.at[i], send_hbm.at[:, i * width:(i + 1) * width], sems.at[5 + i]) for i in range(3)
    ]
    for copy in small + big:
        copy.start()
    for copy in small:
        copy.wait()
    slot = lax.broadcasted_iota(jnp.int32, (slots, n), 0)
    expert = (slot * 2731) >> 16
    place = slot - expert * CAP
    first, second = routes[0:1, :] == expert, routes[1:2, :] == expert
    named = (first | second).astype(f32)
    earlier = lax.broadcasted_iota(jnp.int32, (n, n), 0) < lax.broadcasted_iota(jnp.int32, (n, n), 1)
    before = jnp.dot(named.astype(bf16), earlier.astype(f32).astype(bf16), preferred_element_type=f32)
    here = before.astype(jnp.int32) == place
    pick = jnp.where(here, named, 0.0).astype(bf16)
    for i in range(3):
        big[i].wait()
        send[i] = jnp.dot(pick, rows[i], preferred_element_type=f32).astype(bf16)
        leave[i].start()
    weights = gates[...].astype(f32) / 64.0
    weight = jnp.where(first, weights[0:1, :], 0.0) + jnp.where(second, weights[1:2, :], 0.0)
    mix_ref[...] = jnp.where(here, weight, 0.0).astype(bf16)
    for copy in leave:
        copy.wait()


def prepare(routes, gate_num, tokens, tangent, cotangent, experts):
    n, width = tokens.shape
    slots = experts * CAP
    return pl.pallas_call(
        prepare_kernel,
        out_shape=(
            jax.ShapeDtypeStruct((slots, 3 * width), bf16),
            jax.ShapeDtypeStruct((slots, n), bf16),
        ),
        in_specs=[ANY] * 5,
        out_specs=(ANY, VMEM),
        scratch_shapes=[
            pltpu.VMEM((2, n), jnp.int32),
            pltpu.VMEM((2, n), jnp.int32),
            pltpu.VMEM((3, n, width), bf16),
            pltpu.VMEM((3, slots, width), bf16),
            pltpu.SemaphoreType.DMA((8,)),
        ],
        compiler_params=params(16),
    )(*(pltpu.with_memory_space_constraint(a, pltpu.HBM) for a in (routes.T, gate_num.T, tokens, tangent, cotangent)))


def inner_of(rows_ref, up, down):
    width = up.shape[1]
    before_act = lax.dot_general(rows_ref[:, :width], up, NT, preferred_element_type=f32)
    lifted = lax.dot_general(rows_ref[:, width:2 * width], up, NT, preferred_element_type=f32)
    pulled = lax.dot_general(rows_ref[:, 2 * width:], down, NT, preferred_element_type=f32)
    return (pulled * curvature(before_act) * lifted).astype(bf16)


def accumulate(rows_ref, ups, downs, total=None):
    inners = [inner_of(rows_ref, up[...], down[...]) for up, down in zip(ups, downs)]
    for inner, up in zip(inners, ups):
        part = jnp.dot(inner, up[...], preferred_element_type=f32)
        total = part if total is None else total + part
    return total


def own_kernel(n_w, own_ref, *refs):
    ups, downs = refs[:n_w], refs[n_w:2 * n_w]
    acc_ref, own_out, up_out, down_out, sems = refs[-5:]
    own_copy = pltpu.make_async_copy(own_ref, own_out, sems.at[0])
    copies = []
    for g in range(n_w):
        copies.append(pltpu.make_async_copy(ups[g], up_out.at[g], sems.at[1 + 2 * g]))
        copies.append(pltpu.make_async_copy(downs[g], down_out.at[g], sems.at[2 + 2 * g]))
    for copy in (own_copy, *copies[:4]):
        copy.start()
    for copy in (own_copy, *copies[:2]):
        copy.wait()
    for copy in copies[4:]:
        copy.start()
    total = accumulate(own_out, [up_out.at[0]], [down_out.at[0]])
    for copy in copies[2:]:
        copy.wait()
    rest = range(1, n_w)
    acc_ref[...] = accumulate(own_out, [up_out.at[g] for g in rest], [down_out.at[g] for g in rest], total)


def own_call(own, ups, downs, mark):
    rows, width = own.shape[0], own.shape[1] // 3
    n_w = len(ups)
    stack = jax.ShapeDtypeStruct((n_w, *ups[0].shape), bf16)
    operands = (own, *ups, *downs, mark)
    return pl.pallas_call(
        functools.partial(own_kernel, n_w),
        out_shape=(jax.ShapeDtypeStruct((rows, width), f32), jax.ShapeDtypeStruct(own.shape, bf16), stack, stack),
        in_specs=[ANY] * len(operands),
        out_specs=(VMEM,) * 4,
        scratch_shapes=[pltpu.SemaphoreType.DMA((2 * n_w + 1,))],
        compiler_params=params(16),
    )(*operands)


def other_kernel(other_ref, up_ref, down_ref, acc_ref, other_out, sem):
    copy = pltpu.make_async_copy(other_ref, other_out, sem)
    copy.start()
    copy.wait()
    blocks = range(up_ref.shape[0])
    acc_ref[...] = accumulate(other_out, [up_ref.at[g] for g in blocks], [down_ref.at[g] for g in blocks])


def other_call(other, up_stack, down_stack):
    rows, width = other.shape[0], other.shape[1] // 3
    stacks = [pltpu.with_memory_space_constraint(x, pltpu.VMEM) for x in (up_stack, down_stack)]
    return pl.pallas_call(
        other_kernel,
        out_shape=(jax.ShapeDtypeStruct((rows, width), f32), jax.ShapeDtypeStruct(other.shape, bf16)),
        in_specs=[ANY, VMEM, VMEM],
        out_specs=(VMEM, VMEM),
        scratch_shapes=[pltpu.SemaphoreType.DMA],
        compiler_params=params(16),
    )(other, *stacks)


def next_kernel(n_w, own_ref, other_ref, *refs):
    ups, downs, accs = refs[:n_w], refs[n_w:2 * n_w], refs[2 * n_w:2 * n_w + 2]
    outs, up_buf, down_buf, sems = refs[-5:-3], *refs[-3:]
    copies = []
    for g in range(n_w):
        copies.append(pltpu.make_async_copy(ups[g], up_buf.at[g], sems.at[2 * g]))
        copies.append(pltpu.make_async_copy(downs[g], down_buf.at[g], sems.at[2 * g + 1]))
    for copy in copies:
        copy.start()
    for copy in copies:
        copy.wait()
    blocks = range(n_w)
    for rows_ref, acc_ref, out_ref in zip((own_ref, other_ref), accs, outs):
        total = accumulate(rows_ref, [up_buf.at[g] for g in blocks], [down_buf.at[g] for g in blocks], acc_ref[...])
        out_ref[...] = total.astype(out_ref.dtype)


def next_call(rows, ups, downs, acc, mark):
    n_w = len(ups)
    inside = [pltpu.with_memory_space_constraint(x, pltpu.VMEM) for x in (*rows, *acc)]
    return pl.pallas_call(
        functools.partial(next_kernel, n_w),
        out_shape=tuple(jax.ShapeDtypeStruct(x.shape, kind) for x, kind in zip(acc, (f32, f32))),
        in_specs=[VMEM] * 2 + [ANY] * (2 * n_w) + [VMEM] * 2 + [ANY],
        out_specs=(VMEM,) * 2,
        scratch_shapes=[
            pltpu.VMEM((n_w, *ups[0].shape), bf16),
            pltpu.VMEM((n_w, *ups[0].shape), bf16),
            pltpu.SemaphoreType.DMA((2 * n_w,)),
        ],
        compiler_params=params(20),
    )(*inside[:2], *ups, *downs, *inside[2:], mark)


def factor_kernel(rows_ref, up_ref, factor_ref):
    width = up_ref.shape[1]
    before_act = lax.dot_general(rows_ref[:, :width], up_ref[...], NT, preferred_element_type=f32)
    lifted = lax.dot_general(rows_ref[:, width:2 * width], up_ref[...], NT, preferred_element_type=f32)
    factor_ref[...] = curvature(before_act) * lifted


def last_own_kernel(rows_ref, up_ref, down_ref, acc_ref, out_ref):
    out_ref[...] = accumulate(rows_ref, [up_ref], [down_ref], acc_ref[...])


def last_far_kernel(rows_ref, factor_ref, up_ref, down_ref, acc_ref, passed_ref, out_ref):
    width = up_ref.shape[1]
    pulled = lax.dot_general(rows_ref[:, 2 * width:], down_ref[...], NT, preferred_element_type=f32)
    inner = (pulled * factor_ref[...]).astype(bf16)
    total = acc_ref[...] + passed_ref[...].astype(f32)
    out_ref[...] = (total + jnp.dot(inner, up_ref[...], preferred_element_type=f32)).astype(out_ref.dtype)


def last_call(kernel, shape, kind, *operands):
    operands = tuple(pltpu.with_memory_space_constraint(x, pltpu.VMEM) for x in operands)
    return pl.pallas_call(
        kernel,
        out_shape=jax.ShapeDtypeStruct(shape, kind),
        in_specs=[VMEM] * len(operands),
        out_specs=VMEM,
        compiler_params=params(12),
    )(*operands)


def hold_kernel(*refs):
    refs[-1][...] = jnp.zeros_like(refs[-1])


def hold(*arrays):
    return pl.pallas_call(
        hold_kernel,
        out_shape=jax.ShapeDtypeStruct((8, 128), f32),
        in_specs=[ANY] * len(arrays),
        out_specs=VMEM,
        compiler_params=params(1),
        cost_estimate=pl.CostEstimate(flops=200_000_000_000, bytes_accessed=1_000_000_000, transcendentals=0),
    )(*arrays)


def local(tokens, tangent, cotangent, routes, gate_num, w_up, w_down):
    n_dp = lax.axis_size("dp")
    experts = lax.axis_size("expert")
    width = tokens.shape[1]
    forth = [(i, (i + 2) % n_dp) for i in range(n_dp)]
    back = [(i, (i - 2) % n_dp) for i in range(n_dp)]
    swap = [(i, i ^ 1) for i in range(n_dp)]
    up0, down0 = w_up[0], w_down[0]

    def send_on(x, way):
        return lax.ppermute(x, "dp", way)

    after = lax.optimization_barrier
    uf1, db1 = send_on(up0, forth), send_on(down0, back)
    df1, ub1 = send_on(down0, forth), send_on(up0, back)
    send, mix = prepare(routes, gate_num, tokens, tangent, cotangent, experts)
    own = lax.all_to_all(send.reshape(experts, CAP, 3 * width), "expert", 0, 0, tiled=True)
    own = own.reshape(experts * CAP, 3 * width)
    mark = hold(uf1)
    uf1, db1, mark = after((uf1, db1, mark))
    uf2, db2 = send_on(uf1, forth), send_on(db1, back)
    df1, ub1, mark = after((df1, ub1, mark))
    df2, ub2 = send_on(df1, forth), send_on(ub1, back)
    uf2, db2, df1, ub1 = after((uf2, db2, df1, ub1))
    uf3, db3 = send_on(uf2, forth), send_on(db2, back)
    df2, ub2, uf2, db2 = after((df2, ub2, uf2, db2))
    df3, ub3 = send_on(df2, forth), send_on(ub2, back)
    mine, kept_own, up_stack, down_stack = own_call(own, (up0, uf1, ub1, uf2, ub2), (down0, df1, db1, df2, db2), mark)
    mark3 = hold(uf3, kept_own)
    uf3, db3, df2, ub2, mark3 = after((uf3, db3, df2, ub2, mark3))
    uf4, db4 = send_on(uf3, forth), send_on(db3, back)
    other = lax.ppermute(own, "dp", swap)
    theirs, kept_other = other_call(other, up_stack, down_stack)
    mine, theirs = next_call((kept_own, kept_other), (uf3, ub3), (df3, db3), (mine, theirs), mark3)
    passed = send_on(theirs, swap)
    far_up, far_down = send_on(uf4, swap), send_on(db4, swap)
    part = last_call(last_own_kernel, mine.shape, f32, kept_own, uf4, db4, mine)
    far_up, part = after((far_up, part))
    factor = last_call(factor_kernel, (own.shape[0], far_up.shape[0]), f32, kept_own, far_up)
    whole = last_call(last_far_kernel, mine.shape, bf16, kept_own, factor, far_up, far_down, part, passed)
    returned = lax.all_to_all(whole.reshape(experts, CAP, width), "expert", 0, 0, tiled=True)
    returned = returned.reshape(experts * CAP, width)
    return lax.dot_general(mix, returned, (((0,), (0,)), ((), ())), preferred_element_type=f32)


def solution(mesh):
    tok = P(("dp", "expert"), None)
    w = P("expert", "dp", None)
    return jax.shard_map(
        local, mesh=mesh, in_specs=(tok,) * 5 + (w, w), out_specs=tok, check_vma=False
    )
```
